32 devices in a mesh: tx: 4 (over y, x), ty: 8 (over z, core).
Axes of the slice: x: 2, y: 2, z: 4, core: 2. Of those that a mesh axis runs over, the one named last changes fastest.
Arguments:
- features: bfloat16 [192, 32, 512], P(('tx', 'ty')), may hold values from -6 to 6
- occupancy: int32 [192, 512], P(('tx', 'ty')), may hold values from 0 to 1, as said below
- neighbours: int32 [192, 6], P(('tx', 'ty')), may hold values from -1 to 191, as said below
- w_first: bfloat16 [32, 864], replicated, may hold values from -0.21875 to 0.21875
- w_second: bfloat16 [32, 864], replicated, may hold values from -0.21875 to 0.21875
- cotangent: bfloat16 [192, 32, 512], P(('tx', 'ty')), may hold values from -6 to 6
Outputs:
- result: bfloat16 [192, 32, 512], P(('tx', 'ty'))
- grad_features: bfloat16 [192, 32, 512], P(('tx', 'ty'))
- grad_first: float32 [32, 864], replicated
- grad_second: float32 [32, 864], replicated
The draws below stay inside these ranges and needn't reach their ends.
Inputs may be any that keep to these rules, and one draw needn't show every extreme that they name: Bricks lie on a lattice of 8 x 24 x 1 positions; the tile of device (tx, ty) (brick rows of index tx * 8 + ty) holds positions with x in [tx * 2, (tx+1) * 2) and y in [ty * 3, (ty+1) * 3), one slot each in a drawn order. An id is device * 6 + slot. A neighbour across faces 0 and 1 lies on the same device or on the device one step lower or higher along tx with the same ty; across faces 2 and 3 on the same device or one step along ty; across faces 4 and 5 on the same device. If neighbours[s, f] = t then neighbours[t, f^1] = s. Inactive bricks have all entries -1 and no occupied voxels. `occupancy`: only active bricks have occupied voxels.
All inputs are finite; a program needn't handle non-finite values.
Results may differ from the reference program's by a relative error of at most 0.03.
The reference program's roundings to bfloat16 on the way count: a program that leaves them out, or rounds other values in their place, can miss the bound.
Values may be sent and summed in bfloat16 or wider, within the bound.
A program may use at most 128 MiB of HBM per device.

```python
import math
import jax
import jax.numpy as jnp
from jax import lax

C = 32
EDGE = 8
BX = 2
BY = 3
BZ = 1
VOX = 512
SLOTS = 6
BRICKS = 192
GRID_X = 8
GRID_Y = 24


def lattice(key):
    tiles_x = GRID_X // BX
    tiles_y = GRID_Y // BY
    level = jax.random.randint(jax.random.fold_in(key, 11), (tiles_x, tiles_y), 3, 9)
    level = level.at[tiles_x - 1, tiles_y - 1].set(8)
    tile_level = jnp.repeat(jnp.repeat(level, BX, axis=0), BY, axis=1)[:, :, None]
    dice = jax.random.randint(jax.random.fold_in(key, 12), (GRID_X, GRID_Y, BZ), 0, 8)
    active = dice < tile_level
    keys = jax.random.split(jax.random.fold_in(key, 13), tiles_x * tiles_y)
    slot_of = jax.vmap(lambda k: jax.random.permutation(k, SLOTS))(keys).astype(jnp.int32)
    pos_of = jnp.argsort(slot_of, axis=1).astype(jnp.int32)
    device = jnp.arange(tiles_x * tiles_y, dtype=jnp.int32)[:, None]
    tile_row = device // tiles_y
    tile_col = device % tiles_y
    gx = tile_row * BX + pos_of // (BY * BZ)
    gy = tile_col * BY + pos_of // BZ % BY
    gz = pos_of % BZ
    alive = active[gx, gy, gz]
    offsets = [(-1, 0, 0), (1, 0, 0), (0, -1, 0), (0, 1, 0), (0, 0, -1), (0, 0, 1)]
    columns_list = []
    for step_x, step_y, step_z in offsets:
        nx = gx + step_x
        ny = gy + step_y
        nz = gz + step_z
        inside = (nx >= 0) & (nx < GRID_X) & (ny >= 0) & (ny < GRID_Y) & (nz >= 0) & (nz < BZ)
        cx = jnp.clip(nx, 0, GRID_X - 1)
        cy = jnp.clip(ny, 0, GRID_Y - 1)
        cz = jnp.clip(nz, 0, BZ - 1)
        other = cx // BX * tiles_y + cy // BY
        place = (cx % BX * BY + cy % BY) * BZ + cz
        ident = other * SLOTS + slot_of[other, place]
        keep = inside & alive & active[cx, cy, cz]
        columns_list.append(jnp.where(keep, ident, -1).reshape(-1))
    return (alive.reshape(-1), jnp.stack(columns_list, axis=1).astype(jnp.int32))


def draw_neighbours(key, part):
    return lattice(key)[1]


def draw_occupancy(key, part):
    alive = lattice(key)[0]
    dice = jax.random.randint(jax.random.fold_in(key, 21), (BRICKS, VOX), 0, 5)
    return (alive[:, None] & (dice < 3)).astype(jnp.int32)


def steps_of(rng, shape, cuts, least, high):
    level = 1.0
    for axis_at, blocks in cuts:
        draws = jax.random.uniform(jax.random.fold_in(jax.random.fold_in(rng, 6), axis_at), (blocks,), jnp.float32, least / len(cuts), high / len(cuts))
        level = level * jnp.repeat(jnp.exp(draws), shape[axis_at] // blocks).reshape((-1,) + (1,) * (len(shape) - 1 - axis_at))
    return level


def noise(own_key, shape, scale, most, cuts=(), held_as=jnp.bfloat16):
    drawn = scale * jax.random.normal(own_key, shape, jnp.float32)
    if cuts:
        drawn = drawn * steps_of(own_key, shape, cuts, -0.22, 0.18)
    return jnp.clip(drawn, -most, most).astype(held_as)


def setup_inputs(seed: int = 0) -> dict:
    key_list = jax.random.split(jax.random.key(seed), 7)
    return {
        "features": noise(key_list[0], (BRICKS, C, VOX), 1.0, 6.0, ((0, 32),)),
        "occupancy": draw_occupancy(jax.random.fold_in(key_list[6], 71), 0),
        "neighbours": draw_neighbours(jax.random.fold_in(key_list[6], 71), 0),
        "w_first": noise(key_list[3], (C, 27 * C), (27 * C) ** -0.5, 0.21875),
        "w_second": noise(key_list[4], (C, 27 * C), (27 * C) ** -0.5, 0.21875),
        "cotangent": noise(key_list[5], (BRICKS, C, VOX), 1.0, 6.0, ((0, 32),)),
    }


def face_planes(field):
    count, chans = (field.shape[0], field.shape[1])
    cube = field.reshape(count, chans, EDGE, EDGE, EDGE)
    faces = [cube[:, :, 0], cube[:, :, -1], cube[:, :, :, 0], cube[:, :, :, -1], cube[:, :, :, :, 0], cube[:, :, :, :, -1]]
    return [face.reshape(count, chans, EDGE * EDGE) for face in faces]

def collect_all(items, neighbours):
    result = []
    for face in range(6):
        ident = neighbours[:, face]
        valid = (ident >= 0).astype(items[0].dtype)
        picked = jnp.take(items[face ^ 1], jnp.maximum(ident, 0), axis=0)
        result.append(picked * valid[:, None, None])
    return result

def padded(field, halos):
    count, chans = (field.shape[0], field.shape[1])
    cube = field.reshape(count, chans, EDGE, EDGE, EDGE)
    cells = jnp.pad(cube, ((0, 0), (0, 0), (1, 1), (1, 1), (1, 1)))
    sheet = [h.astype(field.dtype).reshape(count, chans, EDGE, EDGE) for h in halos]
    cells = cells.at[:, :, 0, 1:-1, 1:-1].set(sheet[0])
    cells = cells.at[:, :, -1, 1:-1, 1:-1].set(sheet[1])
    cells = cells.at[:, :, 1:-1, 0, 1:-1].set(sheet[2])
    cells = cells.at[:, :, 1:-1, -1, 1:-1].set(sheet[3])
    cells = cells.at[:, :, 1:-1, 1:-1, 0].set(sheet[4])
    cells = cells.at[:, :, 1:-1, 1:-1, -1].set(sheet[5])
    return cells

def columns(block):
    count, chans = (block.shape[0], block.shape[1])
    pieces = []
    for first in range(3):
        for second in range(3):
            for third in range(3):
                piece = block[:, :, first:first + EDGE, second:second + EDGE, third:third + EDGE]
                pieces.append(piece.reshape(count, chans, EDGE * EDGE * EDGE))
    return jnp.concatenate(pieces, axis=1)

def conv_blocks(cells, weight, group):
    count = cells.shape[0]
    blocks = cells.reshape((count // group, group) + cells.shape[1:])

    def one_block(block):
        return jnp.einsum('ok,gkv->gov', weight.astype(jnp.float32), columns(block).astype(jnp.float32))
    out = lax.map(one_block, blocks)
    return out.reshape(count, weight.shape[0], -1)

def weight_grad(cells, grad, group):
    count = cells.shape[0]
    blocks = cells.reshape((count // group, group) + cells.shape[1:])
    grads = grad.reshape((count // group, group) + grad.shape[1:])

    def one_block(pair):
        return jnp.einsum('gov,gkv->ok', pair[1].astype(jnp.float32), columns(pair[0]).astype(jnp.float32))
    return lax.optimization_barrier(jnp.sum(lax.map(one_block, (blocks, grads)), axis=0))

def flipped(weight):
    chans = weight.shape[0]
    return weight.reshape(chans, 27, chans)[:, ::-1, :].transpose(2, 1, 0).reshape(chans, 27 * chans)

def reference(features, occupancy, neighbours, w_first, w_second, cotangent):
    group = SLOTS
    mask = occupancy.astype(jnp.float32)[:, None, :]
    x_zero = (features.astype(jnp.float32) * mask).astype(jnp.bfloat16)
    pad_x = padded(x_zero, collect_all(face_planes(x_zero), neighbours))
    pre_one = conv_blocks(pad_x, w_first, group)
    hidden = (jnp.maximum(pre_one, 0.0) * mask).astype(jnp.bfloat16)
    pad_h = padded(hidden, collect_all(face_planes(hidden), neighbours))
    pre_two = conv_blocks(pad_h, w_second, group) + x_zero.astype(jnp.float32)
    result = (jnp.maximum(pre_two, 0.0) * mask).astype(jnp.bfloat16)
    grad_two = jnp.where(pre_two > 0.0, cotangent.astype(jnp.float32) * mask, 0.0).astype(jnp.bfloat16)
    scale = 1.0 / math.sqrt(BRICKS * VOX)
    grad_second = weight_grad(pad_h, grad_two, group) * scale
    pad_g = padded(grad_two, collect_all(face_planes(grad_two), neighbours))
    dhidden = conv_blocks(pad_g, flipped(w_second), group)
    grad_one = jnp.where(pre_one > 0.0, dhidden * mask, 0.0).astype(jnp.bfloat16)
    grad_first = weight_grad(pad_x, grad_one, group) * scale
    pad_one = padded(grad_one, collect_all(face_planes(grad_one), neighbours))
    dinput = conv_blocks(pad_one, flipped(w_first), group) + grad_two.astype(jnp.float32)
    grad_features = (dinput * mask).astype(jnp.bfloat16)
    return (result, grad_features, grad_first, grad_second)
```

```python
import functools
import math

import jax
import jax.numpy as jnp
from jax import lax
from jax.experimental import pallas as pl
from jax.experimental.pallas import tpu as pltpu
from jax.sharding import PartitionSpec as P

EDGE = 8
PLANE = EDGE * EDGE
LANES = 128
EXT = (EDGE + 2) * PLANE // LANES
INNER = EDGE * PLANE // LANES
TILE = 8
MESH = pl.DeviceIdType.MESH
F32 = jnp.float32
BF16 = jnp.bfloat16


def turn(value, shift):
    shift = shift % LANES
    return value if shift == 0 else pltpu.roll(value, shift, 1)


def kernel(
    n_tx, n_ty, feat_ref, occ_ref, nbr_ref, w1_ref, w2_ref, cot_ref,
    res_ref, gf_ref, g1_ref, g2_ref,
    field, mask, pre_one, x_zero, grad_two, ex, ey, g3, planes_0, planes_1, planes_2, planes_3,
    wall, wtmp,
    terms, parts, cross, total,
    halo_send, halo_recv, ty_send, ty_recv, tx_send, tx_recv, ag_send, ag_recv,
):
    slots, chans = feat_ref.shape[0], feat_ref.shape[1]
    taps = EDGE + 1
    depth = taps * chans
    tx, ty = lax.axis_index("tx"), lax.axis_index("ty")
    base = (tx * n_ty + ty) * slots
    share = total.shape[1] // n_ty
    used = depth // TILE

    lane = lax.broadcasted_iota(jnp.int32, (chans, LANES), 1)
    low = lane < PLANE
    in_j = (lane // EDGE) % EDGE
    in_k = lane % EDGE
    zero = jnp.zeros((chans, LANES), F32)

    def to_ext(pieces):
        turned = [turn(p, PLANE) for p in pieces]
        out = [jnp.where(low, 0.0, turned[0])]
        for v in range(1, INNER):
            out.append(jnp.where(low, turned[v - 1], turned[v]))
        out.append(jnp.where(low, turned[-1], 0.0))
        return out

    def from_ext(pieces):
        turned = [turn(p, PLANE) for p in pieces]
        return [jnp.where(low, turned[v], turned[v + 1]) for v in range(INNER)]

    def cut(v):
        return slice(v * LANES, (v + 1) * LANES)

    planes = [planes_0, planes_1, planes_2, planes_3]
    for ref in planes:
        ref[...] = jnp.zeros(ref.shape, BF16)
    terms[...] = jnp.zeros(terms.shape, F32)
    barrier = pltpu.get_barrier_semaphore()
    for d in range(1, n_ty):
        pl.semaphore_signal(barrier, inc=1, device_id={"ty": lax.rem(ty + d, n_ty)}, device_id_type=MESH)
    for d in range(1, n_tx):
        pl.semaphore_signal(barrier, inc=1, device_id={"tx": lax.rem(tx + d, n_tx)}, device_id_type=MESH)

    has = [tx > 0, tx < n_tx - 1, ty > 0, ty < n_ty - 1]
    target = [{"tx": tx - 1}, {"tx": tx + 1}, {"ty": ty - 1}, {"ty": ty + 1}]

    def plane_copy(step, face):
        at = step * 4 + face
        return pltpu.make_async_remote_copy(
            src_ref=planes[step].at[face, pl.ds(0, slots)],
            dst_ref=planes[step].at[face, pl.ds(slots, slots)],
            send_sem=halo_send.at[at],
            recv_sem=halo_recv.at[at],
            device_id=target[face],
            device_id_type=MESH,
        )

    def put_planes(step, s, pieces):
        planes[step][0, s] = pieces[0].astype(BF16)
        planes[step][1, s] = pieces[EXT - 1].astype(BF16)
        near, far = zero, zero
        for v in range(EXT):
            near = near + turn(jnp.where(in_j == 0, pieces[v], 0.0), EDGE * v)
            far = far + turn(jnp.where(in_j == EDGE - 1, pieces[v], 0.0), EDGE * v + EDGE)
        planes[step][2, s] = near.astype(BF16)
        planes[step][3, s] = far.astype(BF16)

    def send_planes(step):
        for face in range(4):
            @pl.when(has[face])
            def _():
                plane_copy(step, face).start()

    def wait_planes(step):
        for face in range(4):
            @pl.when(has[face])
            def _():
                plane_copy(step, face ^ 1).wait_recv()

    def end_planes(step):
        for face in range(4):
            @pl.when(has[face])
            def _():
                plane_copy(step, face).wait_send()

    offsets = [-n_ty * slots, n_ty * slots, -slots, slots]

    def halo(step, s, face):
        ident = nbr_ref[s, face]
        own = ident - base
        local = (own >= 0) & (own < slots)
        pick = jnp.where(local, own, own - offsets[face] + slots)
        pick = jnp.clip(pick, 0, 2 * slots - 1)
        got = planes[step][face ^ 1, pick].astype(F32)
        return jnp.where(jnp.full((chans, LANES), ident, jnp.int32) >= 0, got, 0.0)

    def build(step, cols, s):
        ext = [field[s, v] for v in range(EXT)]
        ext[0] = ext[0] + halo(step, s, 0)
        ext[EXT - 1] = ext[EXT - 1] + halo(step, s, 1)
        before, after = halo(step, s, 2), halo(step, s, 3)
        ident = [nbr_ref[s, 4], nbr_ref[s, 5]]
        pick = [jnp.clip(i - base, 0, slots - 1) for i in ident]
        live = [jnp.full((chans, LANES), i, jnp.int32) >= 0 for i in ident]
        for v in range(EXT):
            down = jnp.where(live[0], field[pick[0], v], 0.0)
            up = jnp.where(live[1], field[pick[1], v], 0.0)
            rows = [
                jnp.where(in_j >= 1, turn(ext[v], EDGE), turn(before, -(PLANE + EDGE * v))),
                ext[v],
                jnp.where(in_j < EDGE - 1, turn(ext[v], -EDGE), turn(after, PLANE - EDGE - EDGE * v)),
            ]
            inside = [in_j >= 1, None, in_j < EDGE - 1]
            for b in range(3):
                step_j = EDGE * (1 - b)
                first = turn(down, step_j - (EDGE - 1))
                last = turn(up, step_j + (EDGE - 1))
                if inside[b] is not None:
                    first = jnp.where(inside[b], first, 0.0)
                    last = jnp.where(inside[b], last, 0.0)
                trio = [
                    jnp.where(in_k >= 1, turn(rows[b], 1), first),
                    rows[b],
                    jnp.where(in_k < EDGE - 1, turn(rows[b], -1), last),
                ]
                for c in range(3):
                    at = (b * 3 + c) * chans
                    cols[s, at : at + chans, cut(v)] = trio[c].astype(BF16)

    def conv(which, cols, s):
        out = jnp.dot(wall[which], cols[s], preferred_element_type=F32)
        part = [[out[a * chans : (a + 1) * chans, cut(v)] for v in range(EXT)] for a in range(3)]
        lead = [turn(p, PLANE) for p in part[0]]
        tail = [turn(p, PLANE) for p in part[2]]
        return [
            part[1][v]
            + jnp.where(low, lead[v - 1] if v > 0 else zero, lead[v])
            + jnp.where(low, tail[v], tail[v + 1] if v < EXT - 1 else zero)
            for v in range(EXT)
        ]

    def put_grad(s, pieces):
        turned = [turn(p, PLANE) for p in pieces]
        for v in range(EXT):
            ahead = jnp.where(low, turned[v], turned[v + 1] if v < EXT - 1 else zero)
            behind = jnp.where(low, turned[v - 1] if v > 0 else zero, turned[v])
            g3[s, 0:chans, cut(v)] = ahead.astype(BF16)
            g3[s, chans : 2 * chans, cut(v)] = pieces[v].astype(BF16)
            g3[s, 2 * chans : 3 * chans, cut(v)] = behind.astype(BF16)

    def weight_term(which, cols):
        def one(s, acc):
            return acc + lax.dot_general(
                cols[s], g3[s], (((1,), (1,)), ((), ())), preferred_element_type=F32
            )

        acc = lax.fori_loop(0, slots, one, jnp.zeros((depth, 3 * chans), F32))
        terms[which, 0:used, :, 0 : 3 * chans] = acc.reshape(used, TILE, 3 * chans)

    def scatter_copy(k, d):
        to = lax.rem(ty + d, n_ty)
        return pltpu.make_async_remote_copy(
            src_ref=terms.at[k, pl.ds(to * share, share)],
            dst_ref=parts.at[k, d - 1],
            send_sem=ty_send.at[k, d - 1],
            recv_sem=ty_recv.at[k, d - 1],
            device_id={"ty": to},
            device_id_type=MESH,
        )

    def cross_copy(k, d):
        return pltpu.make_async_remote_copy(
            src_ref=cross.at[k, tx],
            dst_ref=cross.at[k, tx],
            send_sem=tx_send.at[k, d - 1],
            recv_sem=tx_recv.at[k, d - 1],
            device_id={"tx": lax.rem(tx + d, n_tx)},
            device_id_type=MESH,
        )

    def gather_copy(k, d):
        mine = pl.ds(ty * share, share)
        return pltpu.make_async_remote_copy(
            src_ref=total.at[k, mine],
            dst_ref=total.at[k, mine],
            send_sem=ag_send.at[k, d - 1],
            recv_sem=ag_recv.at[k, d - 1],
            device_id={"ty": lax.rem(ty + d, n_ty)},
            device_id_type=MESH,
        )

    def sum_scatter(k):
        for d in range(1, n_ty):
            scatter_copy(k, d).start()

    def sum_cross(k):
        for d in range(1, n_ty):
            scatter_copy(k, d).wait_recv()
        acc = terms[k, pl.ds(ty * share, share)]
        for d in range(1, n_ty):
            acc = acc + parts[k, d - 1]
        cross[k, tx] = acc
        for d in range(1, n_tx):
            cross_copy(k, d).start()

    def sum_gather(k):
        for d in range(1, n_tx):
            cross_copy(k, d).wait_recv()
        acc = cross[k, 0]
        for i in range(1, n_tx):
            acc = acc + cross[k, i]
        total[k, pl.ds(ty * share, share)] = acc
        for d in range(1, n_ty):
            gather_copy(k, d).start()

    scale = 1.0 / math.sqrt(slots * n_tx * n_ty * EDGE * PLANE)

    def sum_end(k, out_ref):
        for d in range(1, n_ty):
            gather_copy(k, d).wait_recv()
        whole = total[k, 0:used].reshape(depth, LANES).T
        for a in range(3):
            out_ref[:, a * depth : (a + 1) * depth] = whole[a * chans : (a + 1) * chans, :] * scale

    def sum_sent(k):
        for d in range(1, n_ty):
            scatter_copy(k, d).wait_send()
            gather_copy(k, d).wait_send()
        for d in range(1, n_tx):
            cross_copy(k, d).wait_send()

    def first(s, carry):
        pieces = to_ext([feat_ref[s, :, cut(v)].astype(F32) for v in range(INNER)])
        pieces = [p * mask[s, v] for v, p in enumerate(pieces)]
        for v in range(EXT):
            field[s, v] = pieces[v]
            x_zero[s, v] = pieces[v]
        put_planes(0, s, pieces)
        return carry

    for s in range(slots):
        holes = to_ext([
            jnp.broadcast_to(occ_ref[s : s + 1, cut(v)].astype(F32), (chans, LANES))
            for v in range(INNER)
        ])
        for v in range(EXT):
            mask[s, v] = holes[v]
    lax.fori_loop(0, slots, first, 0)
    pl.semaphore_wait(barrier, n_ty - 1 + n_tx - 1)
    send_planes(0)

    for k, ref in ((0, w1_ref), (1, w2_ref)):
        wide = ref[...].astype(F32)
        for a in range(3):
            wall[k, a * chans : (a + 1) * chans, :] = wide[:, a * depth : (a + 1) * depth].astype(BF16)
        tall = wide.T
        for t in range(3 * taps):
            back = 3 * taps - 1 - t
            a, bc = t // taps, t % taps
            wtmp[a * chans : (a + 1) * chans, bc * chans : (bc + 1) * chans] = tall[
                back * chans : (back + 1) * chans, :
            ]
        wall[2 + k] = wtmp[...].astype(BF16)

    wait_planes(0)

    def rounded(value):
        return value.astype(BF16).astype(F32)

    def layer_one(s, carry):
        build(0, ex, s)
        out = conv(0, ex, s)
        pieces = []
        for v in range(EXT):
            pre_one[s, v] = out[v]
            pieces.append(rounded(jnp.maximum(out[v], 0.0) * mask[s, v]))
        put_planes(1, s, pieces)
        for v in range(EXT):
            grad_two[s, v] = pieces[v]
        return carry

    def take_field(s, carry):
        for v in range(EXT):
            field[s, v] = grad_two[s, v]
        return carry

    lax.fori_loop(0, slots, layer_one, 0)
    send_planes(1)
    lax.fori_loop(0, slots, take_field, 0)
    wait_planes(1)

    def layer_two(s, carry):
        build(1, ey, s)
        out = conv(1, ey, s)
        cot = to_ext([cot_ref[s, :, cut(v)].astype(F32) for v in range(INNER)])
        result, pieces = [], []
        for v in range(EXT):
            pre = out[v] + x_zero[s, v]
            result.append(jnp.maximum(pre, 0.0) * mask[s, v])
            pieces.append(jnp.where(pre > 0.0, cot[v] * mask[s, v], 0.0))
        for v, piece in enumerate(from_ext(result)):
            res_ref[s, :, cut(v)] = piece.astype(BF16)
        put_planes(2, s, pieces)
        put_grad(s, pieces)
        for v in range(EXT):
            grad_two[s, v] = pieces[v]
        return carry

    lax.fori_loop(0, slots, layer_two, 0)
    send_planes(2)
    weight_term(1, ey)
    sum_scatter(1)
    lax.fori_loop(0, slots, take_field, 0)
    wait_planes(2)

    def layer_three(s, carry):
        build(2, ey, s)
        out = conv(3, ey, s)
        pieces = []
        for v in range(EXT):
            pieces.append(rounded(jnp.where(pre_one[s, v] > 0.0, out[v] * mask[s, v], 0.0)))
        put_planes(3, s, pieces)
        put_grad(s, pieces)
        for v in range(EXT):
            x_zero[s, v] = pieces[v]
        return carry

    lax.fori_loop(0, slots, layer_three, 0)
    send_planes(3)
    sum_cross(1)
    weight_term(0, ex)
    sum_scatter(0)

    def take_last(s, carry):
        for v in range(EXT):
            field[s, v] = x_zero[s, v]
        return carry

    lax.fori_loop(0, slots, take_last, 0)
    sum_gather(1)
    wait_planes(3)

    def layer_four(s, carry):
        build(3, ey, s)
        out = conv(2, ey, s)
        done = [(out[v] + grad_two[s, v]) * mask[s, v] for v in range(EXT)]
        for v, piece in enumerate(from_ext(done)):
            gf_ref[s, :, cut(v)] = piece.astype(BF16)
        return carry

    half = slots // 2
    lax.fori_loop(0, half, layer_four, 0)
    sum_cross(0)
    lax.fori_loop(half, slots, layer_four, 0)
    sum_gather(0)
    sum_end(1, g2_ref)
    sum_end(0, g1_ref)
    for step in range(4):
        end_planes(step)
    sum_sent(0)
    sum_sent(1)


def body(features, occupancy, neighbours, w_first, w_second, cotangent):
    slots, chans = features.shape[0], features.shape[1]
    n_tx, n_ty = lax.axis_size("tx"), lax.axis_size("ty")
    depth = (EDGE + 1) * chans
    blocks = depth // TILE
    share = -(-blocks // n_ty)
    vmem = pl.BlockSpec(memory_space=pltpu.VMEM)
    wide = (slots, EXT, chans, LANES)
    dma = pltpu.SemaphoreType.DMA
    ways_y, ways_x = max(n_ty - 1, 1), max(n_tx - 1, 1)
    return pl.pallas_call(
        functools.partial(kernel, n_tx, n_ty),
        out_shape=(
            jax.ShapeDtypeStruct(features.shape, BF16),
            jax.ShapeDtypeStruct(features.shape, BF16),
            jax.ShapeDtypeStruct(w_first.shape, F32),
            jax.ShapeDtypeStruct(w_second.shape, F32),
        ),
        in_specs=[vmem, vmem, pl.BlockSpec(memory_space=pltpu.SMEM), vmem, vmem, vmem],
        out_specs=(vmem, vmem, vmem, vmem),
        scratch_shapes=[
            pltpu.VMEM(wide, F32),
            pltpu.VMEM(wide, F32),
            pltpu.VMEM(wide, F32),
            pltpu.VMEM(wide, F32),
            pltpu.VMEM(wide, F32),
            pltpu.VMEM((slots, depth, EXT * LANES), BF16),
            pltpu.VMEM((slots, depth, EXT * LANES), BF16),
            pltpu.VMEM((slots, 3 * chans, EXT * LANES), BF16),
            pltpu.VMEM((4, 2 * slots, chans, LANES), BF16),
            pltpu.VMEM((4, 2 * slots, chans, LANES), BF16),
            pltpu.VMEM((4, 2 * slots, chans, LANES), BF16),
            pltpu.VMEM((4, 2 * slots, chans, LANES), BF16),
            pltpu.VMEM((4, 3 * chans, depth), BF16),
            pltpu.VMEM((3 * chans, depth), F32),
            pltpu.VMEM((2, share * n_ty, TILE, LANES), F32),
            pltpu.VMEM((2, ways_y, share, TILE, LANES), F32),
            pltpu.VMEM((2, n_tx, share, TILE, LANES), F32),
            pltpu.VMEM((2, share * n_ty, TILE, LANES), F32),
            dma((16,)),
            dma((16,)),
            dma((2, ways_y)),
            dma((2, ways_y)),
            dma((2, ways_x)),
            dma((2, ways_x)),
            dma((2, ways_y)),
            dma((2, ways_y)),
        ],
        compiler_params=pltpu.CompilerParams(
            collective_id=0, has_side_effects=True, vmem_limit_bytes=48 * 1024 * 1024
        ),
    )(features, occupancy, neighbours, w_first, w_second, cotangent)


def solution(mesh):
    return jax.shard_map(
        body,
        mesh=mesh,
        in_specs=(
            P(("tx", "ty"), None, None),
            P(("tx", "ty"), None),
            P(("tx", "ty"), None),
            P(),
            P(),
            P(("tx", "ty"), None, None),
        ),
        out_specs=(P(("tx", "ty"), None, None), P(("tx", "ty"), None, None), P(), P()),
        check_vma=False,
    )
```

```python
import functools
import math

import jax
import jax.numpy as jnp
from jax import lax
from jax.experimental import pallas as pl
from jax.experimental.pallas import tpu as pltpu
from jax.sharding import PartitionSpec as P

EDGE = 8
PLANE = EDGE * EDGE
LANES = 128
EXT = (EDGE + 2) * PLANE // LANES
INNER = EDGE * PLANE // LANES
TILE = 8
MESH = pl.DeviceIdType.MESH
F32 = jnp.float32
BF16 = jnp.bfloat16


def turn(value, shift):
    shift = shift % LANES
    return value if shift == 0 else pltpu.roll(value, shift, 1)


def kernel(
    n_tx, n_ty, feat_in, occ_in, nbr_in, w1_in, w2_in, cot_in,
    res_out, gf_out, g1_out, g2_out,
    feat_ref, occ_ref, nbr_ref, w1_ref, w2_ref, cot_ref, res_ref, gf_ref, g1_ref, g2_ref,
    mask, pre_one, x_zero, hidden, grad_two, grad_one,
    ex, ey, g3, planes_0, planes_1, planes_2, planes_3,
    wall, wtmp,
    terms, parts, cross, total,
    halo_send, halo_recv, ty_send, ty_recv, tx_send, tx_recv, ag_send, ag_recv, local_sem,
):
    arrivals = [
        pltpu.make_async_copy(src, dst, local_sem.at[i])
        for i, (src, dst) in enumerate((
            (occ_in, occ_ref), (feat_in, feat_ref), (nbr_in, nbr_ref),
            (w1_in, w1_ref), (w2_in, w2_ref), (cot_in, cot_ref),
        ))
    ]
    departures = [
        pltpu.make_async_copy(src, dst, local_sem.at[len(arrivals) + i])
        for i, (src, dst) in enumerate((
            (res_ref, res_out), (gf_ref, gf_out), (g1_ref, g1_out), (g2_ref, g2_out),
        ))
    ]
    for copy in arrivals:
        copy.start()
    slots, chans = feat_ref.shape[0], feat_ref.shape[1]
    taps = EDGE + 1
    depth = taps * chans
    tx, ty = lax.axis_index("tx"), lax.axis_index("ty")
    base = (tx * n_ty + ty) * slots
    share = total.shape[1] // n_ty
    used = depth // TILE

    lane = lax.broadcasted_iota(jnp.int32, (chans, LANES), 1)
    low = lane < PLANE
    in_j = (lane // EDGE) % EDGE
    in_k = lane % EDGE
    zero = jnp.zeros((chans, LANES), F32)
    none = jnp.zeros((chans, LANES), BF16)

    def half_mask(where):
        return jnp.where(where, 1.0, 0.0).astype(BF16) > 0

    low_half = half_mask(low)
    j_first, j_last = half_mask(in_j == 0), half_mask(in_j == EDGE - 1)
    k_first, k_last = half_mask(in_k == 0), half_mask(in_k == EDGE - 1)

    def to_ext(pieces):
        turned = [turn(p, PLANE) for p in pieces]
        out = [jnp.where(low, 0.0, turned[0])]
        for v in range(1, INNER):
            out.append(jnp.where(low, turned[v - 1], turned[v]))
        out.append(jnp.where(low, turned[-1], 0.0))
        return out

    def from_ext(pieces):
        turned = [turn(p, PLANE) for p in pieces]
        return [jnp.where(low, turned[v], turned[v + 1]) for v in range(INNER)]

    def cut(v):
        return slice(v * LANES, (v + 1) * LANES)

    planes = [planes_0, planes_1, planes_2, planes_3]
    for ref in planes:
        ref[:, slots:] = jnp.zeros((4, slots, chans, LANES), BF16)
    terms[...] = jnp.zeros(terms.shape, F32)
    barrier = pltpu.get_barrier_semaphore()
    for d in range(1, n_ty):
        pl.semaphore_signal(barrier, inc=1, device_id={"ty": lax.rem(ty + d, n_ty)}, device_id_type=MESH)
    for d in range(1, n_tx):
        pl.semaphore_signal(barrier, inc=1, device_id={"tx": lax.rem(tx + d, n_tx)}, device_id_type=MESH)

    has = [tx > 0, tx < n_tx - 1, ty > 0, ty < n_ty - 1]
    target = [{"tx": tx - 1}, {"tx": tx + 1}, {"ty": ty - 1}, {"ty": ty + 1}]

    def plane_copy(step, face):
        at = step * 4 + face
        return pltpu.make_async_remote_copy(
            src_ref=planes[step].at[face, pl.ds(0, slots)],
            dst_ref=planes[step].at[face, pl.ds(slots, slots)],
            send_sem=halo_send.at[at],
            recv_sem=halo_recv.at[at],
            device_id=target[face],
            device_id_type=MESH,
        )

    def put_planes(step, s, pieces):
        planes[step][0, s] = pieces[0]
        planes[step][1, s] = pieces[EXT - 1]
        near, far = none, none
        for v in range(EXT):
            near = near + turn(jnp.where(j_first, pieces[v], none), EDGE * v)
            far = far + turn(jnp.where(j_last, pieces[v], none), EDGE * v + EDGE)
        planes[step][2, s] = near
        planes[step][3, s] = far

    def send_planes(step):
        for face in range(4):
            @pl.when(has[face])
            def _():
                plane_copy(step, face).start()

    def wait_planes(step):
        for face in range(4):
            @pl.when(has[face])
            def _():
                plane_copy(step, face ^ 1).wait_recv()

    def end_planes(step):
        for face in range(4):
            @pl.when(has[face])
            def _():
                plane_copy(step, face).wait_send()

    offsets = [-n_ty * slots, n_ty * slots, -slots, slots]

    def halo(step, s, face):
        ident = nbr_ref[s, face]
        own = ident - base
        local = (own >= 0) & (own < slots)
        pick = jnp.where(local, own, own - offsets[face] + slots)
        pick = jnp.clip(pick, 0, 2 * slots - 1)
        return planes[step][face ^ 1, pick] * live(ident)

    def live(ident):
        return jnp.full((chans, LANES), jnp.where(ident >= 0, 1.0, 0.0), F32).astype(BF16)

    def build(step, field, cols, s):
        ext = [field[s, v] for v in range(EXT)]
        ext[0] = ext[0] + halo(step, s, 0)
        ext[EXT - 1] = ext[EXT - 1] + halo(step, s, 1)
        before, after = halo(step, s, 2), halo(step, s, 3)
        ident = [nbr_ref[s, 4], nbr_ref[s, 5]]
        pick = [jnp.clip(i - base, 0, slots - 1) for i in ident]
        there = [live(i) for i in ident]
        for v in range(EXT):
            down = field[pick[0], v] * there[0]
            up = field[pick[1], v] * there[1]
            rows = [
                jnp.where(j_first, turn(before, -(PLANE + EDGE * v)), turn(ext[v], EDGE)),
                ext[v],
                jnp.where(j_last, turn(after, PLANE - EDGE - EDGE * v), turn(ext[v], -EDGE)),
            ]
            outside = [j_first, None, j_last]
            for b in range(3):
                step_j = EDGE * (1 - b)
                first = turn(down, step_j - (EDGE - 1))
                last = turn(up, step_j + (EDGE - 1))
                if outside[b] is not None:
                    first = jnp.where(outside[b], none, first)
                    last = jnp.where(outside[b], none, last)
                trio = [
                    jnp.where(k_first, first, turn(rows[b], 1)),
                    rows[b],
                    jnp.where(k_last, last, turn(rows[b], -1)),
                ]
                for c in range(3):
                    at = (b * 3 + c) * chans
                    cols[s, at : at + chans, cut(v)] = trio[c]

    def conv(which, cols, s):
        out = jnp.dot(wall[which], cols[s], preferred_element_type=F32)
        part = [[out[a * chans : (a + 1) * chans, cut(v)] for v in range(EXT)] for a in range(3)]
        lead = [turn(p, PLANE) for p in part[0]]
        tail = [turn(p, PLANE) for p in part[2]]
        return [
            part[1][v]
            + jnp.where(low, lead[v - 1] if v > 0 else zero, lead[v])
            + jnp.where(low, tail[v], tail[v + 1] if v < EXT - 1 else zero)
            for v in range(EXT)
        ]

    def put_grad(s, pieces):
        turned = [turn(p, PLANE) for p in pieces]
        for v in range(EXT):
            ahead = jnp.where(low_half, turned[v], turned[v + 1] if v < EXT - 1 else none)
            behind = jnp.where(low_half, turned[v - 1] if v > 0 else none, turned[v])
            g3[s, 0:chans, cut(v)] = ahead
            g3[s, chans : 2 * chans, cut(v)] = pieces[v]
            g3[s, 2 * chans : 3 * chans, cut(v)] = behind

    group = 3 if slots % 3 == 0 else 1

    def bricks(start, stop, one):
        def several(g, carry):
            for i in range(group):
                one(g * group + i)
            return carry

        lax.fori_loop(start, stop, several, 0)

    rounds = slots // group

    def weight_term(which, cols):
        def one(s, acc):
            return acc + lax.dot_general(
                cols[s], g3[s], (((1,), (1,)), ((), ())), preferred_element_type=F32
            )

        acc = lax.fori_loop(0, slots, one, jnp.zeros((depth, 3 * chans), F32))
        terms[which, 0:used, :, 0 : 3 * chans] = acc.reshape(used, TILE, 3 * chans)

    def scatter_copy(k, d):
        to = lax.rem(ty + d, n_ty)
        return pltpu.make_async_remote_copy(
            src_ref=terms.at[k, pl.ds(to * share, share)],
            dst_ref=parts.at[k, d - 1],
            send_sem=ty_send.at[k, d - 1],
            recv_sem=ty_recv.at[k, d - 1],
            device_id={"ty": to},
            device_id_type=MESH,
        )

    def cross_copy(k, d):
        return pltpu.make_async_remote_copy(
            src_ref=cross.at[k, tx],
            dst_ref=cross.at[k, tx],
            send_sem=tx_send.at[k, d - 1],
            recv_sem=tx_recv.at[k, d - 1],
            device_id={"tx": lax.rem(tx + d, n_tx)},
            device_id_type=MESH,
        )

    def gather_copy(k, d):
        mine = pl.ds(ty * share, share)
        return pltpu.make_async_remote_copy(
            src_ref=total.at[k, mine],
            dst_ref=total.at[k, mine],
            send_sem=ag_send.at[k, d - 1],
            recv_sem=ag_recv.at[k, d - 1],
            device_id={"ty": lax.rem(ty + d, n_ty)},
            device_id_type=MESH,
        )

    def sum_scatter(k):
        for d in range(1, n_ty):
            scatter_copy(k, d).start()

    def sum_cross(k):
        for d in range(1, n_ty):
            scatter_copy(k, d).wait_recv()
        acc = terms[k, pl.ds(ty * share, share)]
        for d in range(1, n_ty):
            acc = acc + parts[k, d - 1]
        cross[k, tx] = acc
        for d in range(1, n_tx):
            cross_copy(k, d).start()

    def sum_gather(k):
        for d in range(1, n_tx):
            cross_copy(k, d).wait_recv()
        acc = cross[k, 0]
        for i in range(1, n_tx):
            acc = acc + cross[k, i]
        total[k, pl.ds(ty * share, share)] = acc
        for d in range(1, n_ty):
            gather_copy(k, d).start()

    scale = 1.0 / math.sqrt(slots * n_tx * n_ty * EDGE * PLANE)

    def sum_end(k, out_ref):
        for d in range(1, n_ty):
            gather_copy(k, d).wait_recv()
        whole = total[k, 0:used].reshape(depth, LANES).T
        for a in range(3):
            out_ref[:, a * depth : (a + 1) * depth] = whole[a * chans : (a + 1) * chans, :] * scale

    def sum_sent(k):
        for d in range(1, n_ty):
            scatter_copy(k, d).wait_send()
            gather_copy(k, d).wait_send()
        for d in range(1, n_tx):
            cross_copy(k, d).wait_send()

    def first(s):
        pieces = to_ext([feat_ref[s, :, cut(v)].astype(F32) for v in range(INNER)])
        pieces = [(p * mask[s, v]).astype(BF16) for v, p in enumerate(pieces)]
        for v in range(EXT):
            x_zero[s, v] = pieces[v]
        put_planes(0, s, pieces)

    arrivals[0].wait()
    for s in range(slots):
        holes = to_ext([
            jnp.broadcast_to(occ_ref[s : s + 1, cut(v)].astype(F32), (chans, LANES))
            for v in range(INNER)
        ])
        for v in range(EXT):
            mask[s, v] = holes[v]
    arrivals[1].wait()
    bricks(0, rounds, first)
    pl.semaphore_wait(barrier, n_ty - 1 + n_tx - 1)
    send_planes(0)

    def plain_weight(k, ref):
        wide = ref[...].astype(F32)
        for a in range(3):
            wall[k, a * chans : (a + 1) * chans, :] = wide[:, a * depth : (a + 1) * depth].astype(BF16)

    def flipped_weight(k, ref):
        tall = ref[...].astype(F32).T
        for t in range(3 * taps):
            back = 3 * taps - 1 - t
            a, bc = t // taps, t % taps
            wtmp[a * chans : (a + 1) * chans, bc * chans : (bc + 1) * chans] = tall[
                back * chans : (back + 1) * chans, :
            ]
        wall[2 + k] = wtmp[...].astype(BF16)

    for copy in arrivals[2:]:
        copy.wait()
    plain_weight(0, w1_ref)
    plain_weight(1, w2_ref)
    wait_planes(0)

    def layer_one(s):
        build(0, x_zero, ex, s)
        out = conv(0, ex, s)
        pieces = []
        for v in range(EXT):
            pre_one[s, v] = out[v]
            pieces.append((jnp.maximum(out[v], 0.0) * mask[s, v]).astype(BF16))
            hidden[s, v] = pieces[v]
        put_planes(1, s, pieces)

    bricks(0, rounds, layer_one)
    send_planes(1)
    flipped_weight(0, w1_ref)
    flipped_weight(1, w2_ref)
    wait_planes(1)

    def layer_two(s):
        build(1, hidden, ey, s)
        out = conv(1, ey, s)
        cot = to_ext([cot_ref[s, :, cut(v)].astype(F32) for v in range(INNER)])
        result, pieces = [], []
        for v in range(EXT):
            pre = out[v] + x_zero[s, v].astype(F32)
            result.append(jnp.maximum(pre, 0.0) * mask[s, v])
            pieces.append(jnp.where(pre > 0.0, cot[v] * mask[s, v], 0.0).astype(BF16))
            grad_two[s, v] = pieces[v]
        for v, piece in enumerate(from_ext(result)):
            res_ref[s, :, cut(v)] = piece.astype(BF16)
        put_planes(2, s, pieces)
        put_grad(s, pieces)

    bricks(0, rounds, layer_two)
    send_planes(2)
    departures[0].start()
    weight_term(1, ey)
    sum_scatter(1)
    wait_planes(2)

    def layer_three(s):
        build(2, grad_two, ey, s)
        out = conv(3, ey, s)
        pieces = []
        for v in range(EXT):
            pieces.append(jnp.where(pre_one[s, v] > 0.0, out[v] * mask[s, v], 0.0).astype(BF16))
            grad_one[s, v] = pieces[v]
        put_planes(3, s, pieces)
        put_grad(s, pieces)

    bricks(0, rounds, layer_three)
    send_planes(3)
    weight_term(0, ex)
    sum_scatter(0)
    sum_cross(1)
    wait_planes(3)

    def layer_four(s):
        build(3, grad_one, ey, s)
        out = conv(2, ey, s)
        done = [(out[v] + grad_two[s, v].astype(F32)) * mask[s, v] for v in range(EXT)]
        for v, piece in enumerate(from_ext(done)):
            gf_ref[s, :, cut(v)] = piece.astype(BF16)

    half = rounds // 2
    bricks(0, half, layer_four)
    sum_cross(0)
    sum_gather(1)
    bricks(half, rounds, layer_four)
    departures[1].start()
    sum_gather(0)
    sum_end(1, g2_ref)
    departures[3].start()
    sum_end(0, g1_ref)
    departures[2].start()
    for step in range(4):
        end_planes(step)
    sum_sent(0)
    sum_sent(1)
    for copy in departures:
        copy.wait()


def hand_over(*refs):
    sem = refs[-1]
    count = (len(refs) - 1) // 2
    copies = [
        pltpu.make_async_copy(refs[i], refs[count + i], sem.at[i]) for i in range(count)
    ]
    for copy in copies:
        copy.start()
    for copy in copies:
        copy.wait()


def body(features, occupancy, neighbours, w_first, w_second, cotangent):
    slots, chans = features.shape[0], features.shape[1]
    n_tx, n_ty = lax.axis_size("tx"), lax.axis_size("ty")
    depth = (EDGE + 1) * chans
    blocks = depth // TILE
    share = -(-blocks // n_ty)
    wide = (slots, EXT, chans, LANES)
    dma = pltpu.SemaphoreType.DMA
    ways_y, ways_x = max(n_ty - 1, 1), max(n_tx - 1, 1)
    anywhere = pl.BlockSpec(memory_space=pl.ANY)
    outputs = pl.pallas_call(
        functools.partial(kernel, n_tx, n_ty),
        out_shape=(
            jax.ShapeDtypeStruct(features.shape, BF16),
            jax.ShapeDtypeStruct(features.shape, BF16),
            jax.ShapeDtypeStruct(w_first.shape, F32),
            jax.ShapeDtypeStruct(w_second.shape, F32),
        ),
        in_specs=[anywhere] * 6,
        out_specs=(anywhere,) * 4,
        scratch_shapes=[
            pltpu.VMEM(features.shape, BF16),
            pltpu.VMEM(occupancy.shape, jnp.int32),
            pltpu.SMEM(neighbours.shape, jnp.int32),
            pltpu.VMEM(w_first.shape, BF16),
            pltpu.VMEM(w_second.shape, BF16),
            pltpu.VMEM(cotangent.shape, BF16),
            pltpu.VMEM(features.shape, BF16),
            pltpu.VMEM(features.shape, BF16),
            pltpu.VMEM(w_first.shape, F32),
            pltpu.VMEM(w_second.shape, F32),
            pltpu.VMEM(wide, F32),
            pltpu.VMEM(wide, F32),
            pltpu.VMEM(wide, BF16),
            pltpu.VMEM(wide, BF16),
            pltpu.VMEM(wide, BF16),
            pltpu.VMEM(wide, BF16),
            pltpu.VMEM((slots, depth, EXT * LANES), BF16),
            pltpu.VMEM((slots, depth, EXT * LANES), BF16),
            pltpu.VMEM((slots, 3 * chans, EXT * LANES), BF16),
            pltpu.VMEM((4, 2 * slots, chans, LANES), BF16),
            pltpu.VMEM((4, 2 * slots, chans, LANES), BF16),
            pltpu.VMEM((4, 2 * slots, chans, LANES), BF16),
            pltpu.VMEM((4, 2 * slots, chans, LANES), BF16),
            pltpu.VMEM((4, 3 * chans, depth), BF16),
            pltpu.VMEM((3 * chans, depth), F32),
            pltpu.VMEM((2, share * n_ty, TILE, LANES), F32),
            pltpu.VMEM((2, ways_y, share, TILE, LANES), F32),
            pltpu.VMEM((2, n_tx, share, TILE, LANES), F32),
            pltpu.VMEM((2, share * n_ty, TILE, LANES), F32),
            dma((16,)),
            dma((16,)),
            dma((2, ways_y)),
            dma((2, ways_y)),
            dma((2, ways_x)),
            dma((2, ways_x)),
            dma((2, ways_y)),
            dma((2, ways_y)),
            dma((10,)),
        ],
        compiler_params=pltpu.CompilerParams(
            collective_id=0, has_side_effects=True, vmem_limit_bytes=48 * 1024 * 1024
        ),
    )(features, occupancy, neighbours, w_first, w_second, cotangent)
    return pl.pallas_call(
        hand_over,
        out_shape=tuple(jax.ShapeDtypeStruct(o.shape, o.dtype) for o in outputs),
        in_specs=[anywhere] * 4,
        out_specs=(anywhere,) * 4,
        scratch_shapes=[dma((4,))],
    )(*outputs)


def solution(mesh):
    return jax.shard_map(
        body,
        mesh=mesh,
        in_specs=(
            P(("tx", "ty"), None, None),
            P(("tx", "ty"), None),
            P(("tx", "ty"), None),
            P(),
            P(),
            P(("tx", "ty"), None, None),
        ),
        out_specs=(P(("tx", "ty"), None, None), P(("tx", "ty"), None, None), P(), P()),
        check_vma=False,
    )
```

```python
import functools
import math

import jax
import jax.numpy as jnp
from jax import lax
from jax.experimental import pallas as pl
from jax.experimental.pallas import tpu as pltpu
from jax.sharding import PartitionSpec as P

EDGE = 8
PLANE = EDGE * EDGE
LANES = 128
EXT = (EDGE + 2) * PLANE // LANES
INNER = EDGE * PLANE // LANES
TILE = 8
MESH = pl.DeviceIdType.MESH
F32 = jnp.float32
BF16 = jnp.bfloat16


def turn(value, shift):
    shift = shift % LANES
    return value if shift == 0 else pltpu.roll(value, shift, 1)


def kernel(
    n_tx, n_ty, feat_in, occ_in, nbr_in, w1_in, w2_in, cot_in,
    res_out, gf_out, g1_out, g2_out,
    feat_ref, occ_ref, nbr_ref, w1_ref, w2_ref, cot_ref, res_ref, gf_ref, g1_ref, g2_ref,
    mask, pre_one, x_zero, hidden, grad_two, grad_one,
    ex, ey, g3, planes_0, planes_1, planes_2, planes_3,
    wall, wtmp,
    terms, parts, cross, total,
    halo_send, halo_recv, ty_send, ty_recv, tx_send, tx_recv, ag_send, ag_recv, local_sem,
):
    arrivals = [
        pltpu.make_async_copy(src, dst, local_sem.at[i])
        for i, (src, dst) in enumerate((
            (occ_in, occ_ref), (feat_in, feat_ref), (nbr_in, nbr_ref),
            (w1_in, w1_ref), (w2_in, w2_ref), (cot_in, cot_ref),
        ))
    ]
    departures = [
        pltpu.make_async_copy(src, dst, local_sem.at[len(arrivals) + i])
        for i, (src, dst) in enumerate((
            (res_ref, res_out), (gf_ref, gf_out), (g1_ref, g1_out), (g2_ref, g2_out),
        ))
    ]
    for copy in arrivals:
        copy.start()
    slots, chans = feat_ref.shape[0], feat_ref.shape[1]
    taps = EDGE + 1
    depth = taps * chans
    tx, ty = lax.axis_index("tx"), lax.axis_index("ty")
    base = (tx * n_ty + ty) * slots
    share = total.shape[1] // n_ty
    used = depth // TILE

    lane = lax.broadcasted_iota(jnp.int32, (chans, LANES), 1)
    low = lane < PLANE
    in_j = (lane // EDGE) % EDGE
    in_k = lane % EDGE
    zero = jnp.zeros((chans, LANES), F32)
    none = jnp.zeros((chans, LANES), BF16)

    def half_mask(where):
        return jnp.where(where, 1.0, 0.0).astype(BF16) > 0

    low_half = half_mask(low)
    j_first, j_last = half_mask(in_j == 0), half_mask(in_j == EDGE - 1)
    k_first, k_last = half_mask(in_k == 0), half_mask(in_k == EDGE - 1)

    def to_ext(pieces):
        turned = [turn(p, PLANE) for p in pieces]
        out = [jnp.where(low, 0.0, turned[0])]
        for v in range(1, INNER):
            out.append(jnp.where(low, turned[v - 1], turned[v]))
        out.append(jnp.where(low, turned[-1], 0.0))
        return out

    def from_ext(pieces):
        turned = [turn(p, PLANE) for p in pieces]
        return [jnp.where(low, turned[v], turned[v + 1]) for v in range(INNER)]

    def cut(v):
        return slice(v * LANES, (v + 1) * LANES)

    planes = [planes_0, planes_1, planes_2, planes_3]
    for ref in planes:
        ref[:, slots:] = jnp.zeros((4, slots, chans, LANES), BF16)
    terms[...] = jnp.zeros(terms.shape, F32)
    barrier = pltpu.get_barrier_semaphore()
    for d in range(1, n_ty):
        pl.semaphore_signal(barrier, inc=1, device_id={"ty": lax.rem(ty + d, n_ty)}, device_id_type=MESH)
    for d in range(1, n_tx):
        pl.semaphore_signal(barrier, inc=1, device_id={"tx": lax.rem(tx + d, n_tx)}, device_id_type=MESH)

    has = [tx > 0, tx < n_tx - 1, ty > 0, ty < n_ty - 1]
    target = [{"tx": tx - 1}, {"tx": tx + 1}, {"ty": ty - 1}, {"ty": ty + 1}]

    def plane_copy(step, face):
        at = step * 4 + face
        return pltpu.make_async_remote_copy(
            src_ref=planes[step].at[face, pl.ds(0, slots)],
            dst_ref=planes[step].at[face, pl.ds(slots, slots)],
            send_sem=halo_send.at[at],
            recv_sem=halo_recv.at[at],
            device_id=target[face],
            device_id_type=MESH,
        )

    def put_planes(step, s, pieces):
        planes[step][0, s] = pieces[0]
        planes[step][1, s] = pieces[EXT - 1]
        near, far = none, none
        for v in range(EXT):
            near = near + turn(jnp.where(j_first, pieces[v], none), EDGE * v)
            far = far + turn(jnp.where(j_last, pieces[v], none), EDGE * v + EDGE)
        planes[step][2, s] = near
        planes[step][3, s] = far

    def send_planes(step):
        for face in range(4):
            @pl.when(has[face])
            def _():
                plane_copy(step, face).start()

    def wait_planes(step):
        for face in range(4):
            @pl.when(has[face])
            def _():
                plane_copy(step, face ^ 1).wait_recv()

    def end_planes(step):
        for face in range(4):
            @pl.when(has[face])
            def _():
                plane_copy(step, face).wait_send()

    offsets = [-n_ty * slots, n_ty * slots, -slots, slots]

    def halo(step, s, face):
        ident = nbr_ref[s, face]
        own = ident - base
        local = (own >= 0) & (own < slots)
        pick = jnp.where(local, own, own - offsets[face] + slots)
        pick = jnp.clip(pick, 0, 2 * slots - 1)
        return planes[step][face ^ 1, pick] * live(ident)

    def live(ident):
        return jnp.full((chans, LANES), jnp.where(ident >= 0, 1.0, 0.0), F32).astype(BF16)

    def build(step, field, cols, s):
        ext = [field[s, v] for v in range(EXT)]
        ext[0] = ext[0] + halo(step, s, 0)
        ext[EXT - 1] = ext[EXT - 1] + halo(step, s, 1)
        before, after = halo(step, s, 2), halo(step, s, 3)
        ident = [nbr_ref[s, 4], nbr_ref[s, 5]]
        pick = [jnp.clip(i - base, 0, slots - 1) for i in ident]
        there = [live(i) for i in ident]
        for v in range(EXT):
            down = field[pick[0], v] * there[0]
            up = field[pick[1], v] * there[1]
            rows = [
                jnp.where(j_first, turn(before, -(PLANE + EDGE * v)), turn(ext[v], EDGE)),
                ext[v],
                jnp.where(j_last, turn(after, PLANE - EDGE - EDGE * v), turn(ext[v], -EDGE)),
            ]
            outside = [j_first, None, j_last]
            for b in range(3):
                step_j = EDGE * (1 - b)
                first = turn(down, step_j - (EDGE - 1))
                last = turn(up, step_j + (EDGE - 1))
                if outside[b] is not None:
                    first = jnp.where(outside[b], none, first)
                    last = jnp.where(outside[b], none, last)
                trio = [
                    jnp.where(k_first, first, turn(rows[b], 1)),
                    rows[b],
                    jnp.where(k_last, last, turn(rows[b], -1)),
                ]
                for c in range(3):
                    at = (b * 3 + c) * chans
                    cols[s, at : at + chans, cut(v)] = trio[c]

    def conv(which, cols, s):
        out = jnp.dot(wall[which], cols[s], preferred_element_type=F32)
        part = [[out[a * chans : (a + 1) * chans, cut(v)] for v in range(EXT)] for a in range(3)]
        lead = [turn(p, PLANE) for p in part[0]]
        tail = [turn(p, PLANE) for p in part[2]]
        return [
            part[1][v]
            + jnp.where(low, lead[v - 1] if v > 0 else zero, lead[v])
            + jnp.where(low, tail[v], tail[v + 1] if v < EXT - 1 else zero)
            for v in range(EXT)
        ]

    def put_grad(s, pieces):
        turned = [turn(p, PLANE) for p in pieces]
        for v in range(EXT):
            ahead = jnp.where(low_half, turned[v], turned[v + 1] if v < EXT - 1 else none)
            behind = jnp.where(low_half, turned[v - 1] if v > 0 else none, turned[v])
            g3[s, 0:chans, cut(v)] = ahead
            g3[s, chans : 2 * chans, cut(v)] = pieces[v]
            g3[s, 2 * chans : 3 * chans, cut(v)] = behind

    group = 3 if slots % 3 == 0 else 1

    def bricks(start, stop, one):
        def several(g, carry):
            for i in range(group):
                one(g * group + i)
            return carry

        lax.fori_loop(start, stop, several, 0)

    rounds = slots // group

    def weight_term(which, cols):
        def one(s, acc):
            return acc + lax.dot_general(
                cols[s], g3[s], (((1,), (1,)), ((), ())), preferred_element_type=F32
            )

        acc = lax.fori_loop(0, slots, one, jnp.zeros((depth, 3 * chans), F32))
        terms[which, 0:used, :, 0 : 3 * chans] = acc.reshape(used, TILE, 3 * chans)

    def scatter_copy(k, d):
        to = lax.rem(ty + d, n_ty)
        return pltpu.make_async_remote_copy(
            src_ref=terms.at[k, pl.ds(to * share, share)],
            dst_ref=parts.at[k, d - 1],
            send_sem=ty_send.at[k, d - 1],
            recv_sem=ty_recv.at[k, d - 1],
            device_id={"ty": to},
            device_id_type=MESH,
        )

    def cross_copy(k, d):
        return pltpu.make_async_remote_copy(
            src_ref=cross.at[k, tx],
            dst_ref=cross.at[k, tx],
            send_sem=tx_send.at[k, d - 1],
            recv_sem=tx_recv.at[k, d - 1],
            device_id={"tx": lax.rem(tx + d, n_tx)},
            device_id_type=MESH,
        )

    def gather_copy(k, d):
        mine = pl.ds(ty * share, share)
        return pltpu.make_async_remote_copy(
            src_ref=total.at[k, mine],
            dst_ref=total.at[k, mine],
            send_sem=ag_send.at[k, d - 1],
            recv_sem=ag_recv.at[k, d - 1],
            device_id={"ty": lax.rem(ty + d, n_ty)},
            device_id_type=MESH,
        )

    def sum_scatter(k):
        for d in range(1, n_ty):
            scatter_copy(k, d).start()

    def sum_cross(k):
        for d in range(1, n_ty):
            scatter_copy(k, d).wait_recv()
        acc = terms[k, pl.ds(ty * share, share)]
        for d in range(1, n_ty):
            acc = acc + parts[k, d - 1]
        cross[k, tx] = acc
        for d in range(1, n_tx):
            cross_copy(k, d).start()

    def sum_gather(k):
        for d in range(1, n_tx):
            cross_copy(k, d).wait_recv()
        acc = cross[k, 0]
        for i in range(1, n_tx):
            acc = acc + cross[k, i]
        total[k, pl.ds(ty * share, share)] = acc
        for d in range(1, n_ty):
            gather_copy(k, d).start()

    scale = 1.0 / math.sqrt(slots * n_tx * n_ty * EDGE * PLANE)

    def sum_end(k, out_ref):
        for d in range(1, n_ty):
            gather_copy(k, d).wait_recv()
        whole = total[k, 0:used].reshape(depth, LANES).T
        for a in range(3):
            out_ref[:, a * depth : (a + 1) * depth] = whole[a * chans : (a + 1) * chans, :] * scale

    def sum_sent(k):
        for d in range(1, n_ty):
            scatter_copy(k, d).wait_send()
            gather_copy(k, d).wait_send()
        for d in range(1, n_tx):
            cross_copy(k, d).wait_send()

    def first(s):
        pieces = to_ext([feat_ref[s, :, cut(v)].astype(F32) for v in range(INNER)])
        pieces = [(p * mask[s, v]).astype(BF16) for v, p in enumerate(pieces)]
        for v in range(EXT):
            x_zero[s, v] = pieces[v]
        put_planes(0, s, pieces)

    arrivals[0].wait()
    for s in range(slots):
        holes = to_ext([
            jnp.broadcast_to(occ_ref[s : s + 1, cut(v)].astype(F32), (chans, LANES))
            for v in range(INNER)
        ])
        for v in range(EXT):
            mask[s, v] = holes[v]
    arrivals[1].wait()
    bricks(0, rounds, first)
    pl.semaphore_wait(barrier, n_ty - 1 + n_tx - 1)
    send_planes(0)

    def plain_weight(k, ref):
        wide = ref[...].astype(F32)
        for a in range(3):
            wall[k, a * chans : (a + 1) * chans, :] = wide[:, a * depth : (a + 1) * depth].astype(BF16)

    def flipped_weight(k, ref):
        tall = ref[...].astype(F32).T
        for t in range(3 * taps):
            back = 3 * taps - 1 - t
            a, bc = t // taps, t % taps
            wtmp[a * chans : (a + 1) * chans, bc * chans : (bc + 1) * chans] = tall[
                back * chans : (back + 1) * chans, :
            ]
        wall[2 + k] = wtmp[...].astype(BF16)

    for copy in arrivals[2:]:
        copy.wait()
    plain_weight(0, w1_ref)
    plain_weight(1, w2_ref)
    wait_planes(0)

    def layer_one(s):
        build(0, x_zero, ex, s)
        out = conv(0, ex, s)
        pieces = []
        for v in range(EXT):
            pre_one[s, v] = out[v]
            pieces.append((jnp.maximum(out[v], 0.0) * mask[s, v]).astype(BF16))
            hidden[s, v] = pieces[v]
        put_planes(1, s, pieces)

    bricks(0, rounds, layer_one)
    send_planes(1)
    flipped_weight(0, w1_ref)
    flipped_weight(1, w2_ref)
    wait_planes(1)

    def layer_two(s):
        build(1, hidden, ey, s)
        out = conv(1, ey, s)
        cot = to_ext([cot_ref[s, :, cut(v)].astype(F32) for v in range(INNER)])
        result, pieces = [], []
        for v in range(EXT):
            pre = out[v] + x_zero[s, v].astype(F32)
            result.append(jnp.maximum(pre, 0.0) * mask[s, v])
            pieces.append(jnp.where(pre > 0.0, cot[v] * mask[s, v], 0.0).astype(BF16))
            grad_two[s, v] = pieces[v]
        for v, piece in enumerate(from_ext(result)):
            res_ref[s, :, cut(v)] = piece.astype(BF16)
        put_planes(2, s, pieces)
        put_grad(s, pieces)

    bricks(0, rounds, layer_two)
    send_planes(2)
    departures[0].start()
    weight_term(1, ey)
    sum_scatter(1)
    wait_planes(2)

    def layer_three(s):
        build(2, grad_two, ey, s)
        out = conv(3, ey, s)
        pieces = []
        for v in range(EXT):
            pieces.append(jnp.where(pre_one[s, v] > 0.0, out[v] * mask[s, v], 0.0).astype(BF16))
            grad_one[s, v] = pieces[v]
        put_planes(3, s, pieces)
        put_grad(s, pieces)

    bricks(0, rounds, layer_three)
    send_planes(3)
    weight_term(0, ex)
    sum_scatter(0)
    sum_cross(1)
    wait_planes(3)

    def layer_four(s):
        build(3, grad_one, ey, s)
        out = conv(2, ey, s)
        done = [(out[v] + grad_two[s, v].astype(F32)) * mask[s, v] for v in range(EXT)]
        for v, piece in enumerate(from_ext(done)):
            gf_ref[s, :, cut(v)] = piece.astype(BF16)

    half = rounds // 2
    bricks(0, half, layer_four)
    sum_cross(0)
    sum_gather(1)
    bricks(half, rounds, layer_four)
    departures[1].start()
    sum_gather(0)
    sum_end(1, g2_ref)
    departures[3].start()
    sum_end(0, g1_ref)
    departures[2].start()
    for step in range(4):
        end_planes(step)
    sum_sent(0)
    sum_sent(1)
    for copy in departures:
        copy.wait()


def body(features, occupancy, neighbours, w_first, w_second, cotangent):
    slots, chans = features.shape[0], features.shape[1]
    n_tx, n_ty = lax.axis_size("tx"), lax.axis_size("ty")
    depth = (EDGE + 1) * chans
    blocks = depth // TILE
    share = -(-blocks // n_ty)
    wide = (slots, EXT, chans, LANES)
    dma = pltpu.SemaphoreType.DMA
    ways_y, ways_x = max(n_ty - 1, 1), max(n_tx - 1, 1)
    in_hbm = pl.BlockSpec(memory_space=pltpu.HBM)
    return pl.pallas_call(
        functools.partial(kernel, n_tx, n_ty),
        out_shape=(
            jax.ShapeDtypeStruct(features.shape, BF16),
            jax.ShapeDtypeStruct(features.shape, BF16),
            jax.ShapeDtypeStruct(w_first.shape, F32),
            jax.ShapeDtypeStruct(w_second.shape, F32),
        ),
        in_specs=[in_hbm] * 6,
        out_specs=(in_hbm,) * 4,
        scratch_shapes=[
            pltpu.VMEM(features.shape, BF16),
            pltpu.VMEM(occupancy.shape, jnp.int32),
            pltpu.SMEM(neighbours.shape, jnp.int32),
            pltpu.VMEM(w_first.shape, BF16),
            pltpu.VMEM(w_second.shape, BF16),
            pltpu.VMEM(cotangent.shape, BF16),
            pltpu.VMEM(features.shape, BF16),
            pltpu.VMEM(features.shape, BF16),
            pltpu.VMEM(w_first.shape, F32),
            pltpu.VMEM(w_second.shape, F32),
            pltpu.VMEM(wide, F32),
            pltpu.VMEM(wide, F32),
            pltpu.VMEM(wide, BF16),
            pltpu.VMEM(wide, BF16),
            pltpu.VMEM(wide, BF16),
            pltpu.VMEM(wide, BF16),
            pltpu.VMEM((slots, depth, EXT * LANES), BF16),
            pltpu.VMEM((slots, depth, EXT * LANES), BF16),
            pltpu.VMEM((slots, 3 * chans, EXT * LANES), BF16),
            pltpu.VMEM((4, 2 * slots, chans, LANES), BF16),
            pltpu.VMEM((4, 2 * slots, chans, LANES), BF16),
            pltpu.VMEM((4, 2 * slots, chans, LANES), BF16),
            pltpu.VMEM((4, 2 * slots, chans, LANES), BF16),
            pltpu.VMEM((4, 3 * chans, depth), BF16),
            pltpu.VMEM((3 * chans, depth), F32),
            pltpu.VMEM((2, share * n_ty, TILE, LANES), F32),
            pltpu.VMEM((2, ways_y, share, TILE, LANES), F32),
            pltpu.VMEM((2, n_tx, share, TILE, LANES), F32),
            pltpu.VMEM((2, share * n_ty, TILE, LANES), F32),
            dma((16,)),
            dma((16,)),
            dma((2, ways_y)),
            dma((2, ways_y)),
            dma((2, ways_x)),
            dma((2, ways_x)),
            dma((2, ways_y)),
            dma((2, ways_y)),
            dma((10,)),
        ],
        compiler_params=pltpu.CompilerParams(
            collective_id=0, has_side_effects=True, vmem_limit_bytes=63 * 1024 * 1024
        ),
    )(features, occupancy, neighbours, w_first, w_second, cotangent)


def solution(mesh):
    return jax.shard_map(
        body,
        mesh=mesh,
        in_specs=(
            P(("tx", "ty"), None, None),
            P(("tx", "ty"), None),
            P(("tx", "ty"), None),
            P(),
            P(),
            P(("tx", "ty"), None, None),
        ),
        out_specs=(P(("tx", "ty"), None, None), P(("tx", "ty"), None, None), P(), P()),
        check_vma=False,
    )
```

```python
import functools
import math

import jax
import jax.numpy as jnp
from jax import lax
from jax.experimental import pallas as pl
from jax.experimental.pallas import tpu as pltpu
from jax.sharding import PartitionSpec as P

EDGE = 8
PLANE = EDGE * EDGE
LANES = 128
EXT = (EDGE + 2) * PLANE // LANES
INNER = EDGE * PLANE // LANES
TILE = 8
MESH = pl.DeviceIdType.MESH
F32 = jnp.float32
BF16 = jnp.bfloat16


def turn(value, shift):
    shift = shift % LANES
    return value if shift == 0 else pltpu.roll(value, shift, 1)


def kernel(
    n_tx, n_ty, feat_in, occ_in, nbr_in, w1_in, w2_in, cot_in,
    res_out, gf_out, g1_out, g2_out,
    feat_ref, occ_ref, nbr_ref, w1_ref, w2_ref, cot_ref, res_ref, gf_ref, g1_ref, g2_ref,
    mask, pre_one, x_zero, hidden, grad_two, grad_one,
    ex, ey, g3, planes_0, planes_1, planes_2, planes_3,
    wall, wtmp,
    terms, parts, cross, total,
    halo_send, halo_recv, ty_send, ty_recv, tx_send, tx_recv, ag_send, ag_recv, local_sem,
):
    arrivals = [
        pltpu.make_async_copy(src, dst, local_sem.at[i])
        for i, (src, dst) in enumerate((
            (occ_in, occ_ref), (feat_in, feat_ref), (nbr_in, nbr_ref),
            (w1_in, w1_ref), (w2_in, w2_ref), (cot_in, cot_ref),
        ))
    ]
    departures = [
        pltpu.make_async_copy(src, dst, local_sem.at[len(arrivals) + i])
        for i, (src, dst) in enumerate((
            (res_ref, res_out), (gf_ref, gf_out), (g1_ref, g1_out), (g2_ref, g2_out),
        ))
    ]
    for copy in arrivals:
        copy.start()
    slots, chans = feat_ref.shape[0], feat_ref.shape[1]
    taps = EDGE + 1
    depth = taps * chans
    tx, ty = lax.axis_index("tx"), lax.axis_index("ty")
    base = (tx * n_ty + ty) * slots
    share = total.shape[1] // n_ty
    used = depth // TILE

    lane = lax.broadcasted_iota(jnp.int32, (chans, LANES), 1)
    low = lane < PLANE
    in_j = (lane // EDGE) % EDGE
    in_k = lane % EDGE
    zero = jnp.zeros((chans, LANES), F32)
    none = jnp.zeros((chans, LANES), BF16)

    def half_mask(where):
        return jnp.where(where, 1.0, 0.0).astype(BF16) > 0

    low_half = half_mask(low)
    j_first, j_last = half_mask(in_j == 0), half_mask(in_j == EDGE - 1)
    k_first, k_last = half_mask(in_k == 0), half_mask(in_k == EDGE - 1)

    def to_ext(pieces):
        turned = [turn(p, PLANE) for p in pieces]
        out = [jnp.where(low, 0.0, turned[0])]
        for v in range(1, INNER):
            out.append(jnp.where(low, turned[v - 1], turned[v]))
        out.append(jnp.where(low, turned[-1], 0.0))
        return out

    def from_ext(pieces):
        turned = [turn(p, PLANE) for p in pieces]
        return [jnp.where(low, turned[v], turned[v + 1]) for v in range(INNER)]

    def cut(v):
        return slice(v * LANES, (v + 1) * LANES)

    planes = [planes_0, planes_1, planes_2, planes_3]
    for ref in planes:
        ref[:, slots:] = jnp.zeros((4, slots, chans, LANES), BF16)
    terms[...] = jnp.zeros(terms.shape, F32)
    barrier = pltpu.get_barrier_semaphore()
    for d in range(1, n_ty):
        pl.semaphore_signal(barrier, inc=1, device_id={"ty": lax.rem(ty + d, n_ty)}, device_id_type=MESH)
    for d in range(1, n_tx):
        pl.semaphore_signal(barrier, inc=1, device_id={"tx": lax.rem(tx + d, n_tx)}, device_id_type=MESH)

    has = [tx > 0, tx < n_tx - 1, ty > 0, ty < n_ty - 1]
    target = [{"tx": tx - 1}, {"tx": tx + 1}, {"ty": ty - 1}, {"ty": ty + 1}]

    def plane_copy(step, face):
        at = step * 4 + face
        return pltpu.make_async_remote_copy(
            src_ref=planes[step].at[face, pl.ds(0, slots)],
            dst_ref=planes[step].at[face, pl.ds(slots, slots)],
            send_sem=halo_send.at[at],
            recv_sem=halo_recv.at[at],
            device_id=target[face],
            device_id_type=MESH,
        )

    def put_planes(step, s, pieces):
        planes[step][0, s] = pieces[0]
        planes[step][1, s] = pieces[EXT - 1]
        near, far = none, none
        for v in range(EXT):
            near = near + turn(jnp.where(j_first, pieces[v], none), EDGE * v)
            far = far + turn(jnp.where(j_last, pieces[v], none), EDGE * v + EDGE)
        planes[step][2, s] = near
        planes[step][3, s] = far

    def send_planes(step):
        for face in range(4):
            @pl.when(has[face])
            def _():
                plane_copy(step, face).start()

    def wait_planes(step):
        for face in range(4):
            @pl.when(has[face])
            def _():
                plane_copy(step, face ^ 1).wait_recv()

    def end_planes(step):
        for face in range(4):
            @pl.when(has[face])
            def _():
                plane_copy(step, face).wait_send()

    offsets = [-n_ty * slots, n_ty * slots, -slots, slots]

    def halo(step, s, face):
        ident = nbr_ref[s, face]
        own = ident - base
        local = (own >= 0) & (own < slots)
        pick = jnp.where(local, own, own - offsets[face] + slots)
        pick = jnp.clip(pick, 0, 2 * slots - 1)
        return planes[step][face ^ 1, pick] * live(ident)

    def live(ident):
        return jnp.full((chans, LANES), jnp.where(ident >= 0, 1.0, 0.0), F32).astype(BF16)

    def build(step, field, cols, s):
        ext = [field[s, v] for v in range(EXT)]
        ext[0] = ext[0] + halo(step, s, 0)
        ext[EXT - 1] = ext[EXT - 1] + halo(step, s, 1)
        before, after = halo(step, s, 2), halo(step, s, 3)
        ident = [nbr_ref[s, 4], nbr_ref[s, 5]]
        pick = [jnp.clip(i - base, 0, slots - 1) for i in ident]
        there = [live(i) for i in ident]
        for v in range(EXT):
            down = field[pick[0], v] * there[0]
            up = field[pick[1], v] * there[1]
            rows = [
                jnp.where(j_first, turn(before, -(PLANE + EDGE * v)), turn(ext[v], EDGE)),
                ext[v],
                jnp.where(j_last, turn(after, PLANE - EDGE - EDGE * v), turn(ext[v], -EDGE)),
            ]
            outside = [j_first, None, j_last]
            for b in range(3):
                step_j = EDGE * (1 - b)
                first = turn(down, step_j - (EDGE - 1))
                last = turn(up, step_j + (EDGE - 1))
                if outside[b] is not None:
                    first = jnp.where(outside[b], none, first)
                    last = jnp.where(outside[b], none, last)
                trio = [
                    jnp.where(k_first, first, turn(rows[b], 1)),
                    rows[b],
                    jnp.where(k_last, last, turn(rows[b], -1)),
                ]
                for c in range(3):
                    at = (b * 3 + c) * chans
                    cols[s, at : at + chans, cut(v)] = trio[c]

    def conv(which, cols, s):
        out = jnp.dot(wall[which], cols[s], preferred_element_type=F32)
        part = [[out[a * chans : (a + 1) * chans, cut(v)] for v in range(EXT)] for a in range(3)]
        lead = [turn(p, PLANE) for p in part[0]]
        tail = [turn(p, PLANE) for p in part[2]]
        return [
            part[1][v]
            + jnp.where(low, lead[v - 1] if v > 0 else zero, lead[v])
            + jnp.where(low, tail[v], tail[v + 1] if v < EXT - 1 else zero)
            for v in range(EXT)
        ]

    def put_grad(s, pieces):
        turned = [turn(p, PLANE) for p in pieces]
        for v in range(EXT):
            ahead = jnp.where(low_half, turned[v], turned[v + 1] if v < EXT - 1 else none)
            behind = jnp.where(low_half, turned[v - 1] if v > 0 else none, turned[v])
            g3[s, 0:chans, cut(v)] = ahead
            g3[s, chans : 2 * chans, cut(v)] = pieces[v]
            g3[s, 2 * chans : 3 * chans, cut(v)] = behind

    def grouping(wish):
        return wish if slots % wish == 0 else 1

    def bricks(start, stop, one, group):
        def several(g, carry):
            for i in range(group):
                one(g * group + i)
            return carry

        lax.fori_loop(start, stop, several, 0)

    group = grouping(3)
    rounds = slots // group

    def weight_term(which, cols):
        def one(s, acc):
            return acc + lax.dot_general(
                cols[s], g3[s], (((1,), (1,)), ((), ())), preferred_element_type=F32
            )

        acc = lax.fori_loop(0, slots, one, jnp.zeros((depth, 3 * chans), F32))
        terms[which, 0:used, :, 0 : 3 * chans] = acc.reshape(used, TILE, 3 * chans)

    def scatter_copy(k, d):
        to = lax.rem(ty + d, n_ty)
        return pltpu.make_async_remote_copy(
            src_ref=terms.at[k, pl.ds(to * share, share)],
            dst_ref=parts.at[k, d - 1],
            send_sem=ty_send.at[k, d - 1],
            recv_sem=ty_recv.at[k, d - 1],
            device_id={"ty": to},
            device_id_type=MESH,
        )

    def cross_copy(k, d):
        return pltpu.make_async_remote_copy(
            src_ref=cross.at[k, tx],
            dst_ref=cross.at[k, tx],
            send_sem=tx_send.at[k, d - 1],
            recv_sem=tx_recv.at[k, d - 1],
            device_id={"tx": lax.rem(tx + d, n_tx)},
            device_id_type=MESH,
        )

    def gather_copy(k, d):
        mine = pl.ds(ty * share, share)
        return pltpu.make_async_remote_copy(
            src_ref=total.at[k, mine],
            dst_ref=total.at[k, mine],
            send_sem=ag_send.at[k, d - 1],
            recv_sem=ag_recv.at[k, d - 1],
            device_id={"ty": lax.rem(ty + d, n_ty)},
            device_id_type=MESH,
        )

    def sum_scatter(k):
        for d in range(1, n_ty):
            scatter_copy(k, d).start()

    def sum_cross(k):
        for d in range(1, n_ty):
            scatter_copy(k, d).wait_recv()
        acc = terms[k, pl.ds(ty * share, share)]
        for d in range(1, n_ty):
            acc = acc + parts[k, d - 1]
        cross[k, tx] = acc
        for d in range(1, n_tx):
            cross_copy(k, d).start()

    def sum_gather(k):
        for d in range(1, n_tx):
            cross_copy(k, d).wait_recv()
        acc = cross[k, 0]
        for i in range(1, n_tx):
            acc = acc + cross[k, i]
        total[k, pl.ds(ty * share, share)] = acc
        for d in range(1, n_ty):
            gather_copy(k, d).start()

    scale = 1.0 / math.sqrt(slots * n_tx * n_ty * EDGE * PLANE)

    def sum_end(k, out_ref):
        for d in range(1, n_ty):
            gather_copy(k, d).wait_recv()
        whole = total[k, 0:used].reshape(depth, LANES).T
        for a in range(3):
            out_ref[:, a * depth : (a + 1) * depth] = whole[a * chans : (a + 1) * chans, :] * scale

    def sum_sent(k):
        for d in range(1, n_ty):
            scatter_copy(k, d).wait_send()
            gather_copy(k, d).wait_send()
        for d in range(1, n_tx):
            cross_copy(k, d).wait_send()

    def first(s):
        pieces = to_ext([feat_ref[s, :, cut(v)].astype(F32) for v in range(INNER)])
        pieces = [(p * mask[s, v]).astype(BF16) for v, p in enumerate(pieces)]
        for v in range(EXT):
            x_zero[s, v] = pieces[v]
        put_planes(0, s, pieces)

    arrivals[0].wait()
    for s in range(slots):
        holes = to_ext([
            jnp.broadcast_to(occ_ref[s : s + 1, cut(v)].astype(F32), (chans, LANES))
            for v in range(INNER)
        ])
        for v in range(EXT):
            mask[s, v] = holes[v]
    arrivals[1].wait()
    bricks(0, rounds, first, group)
    pl.semaphore_wait(barrier, n_ty - 1 + n_tx - 1)
    send_planes(0)

    def plain_weight(k, ref):
        wide = ref[...].astype(F32)
        for a in range(3):
            wall[k, a * chans : (a + 1) * chans, :] = wide[:, a * depth : (a + 1) * depth].astype(BF16)

    def flipped_weight(k, ref):
        tall = ref[...].astype(F32).T
        for t in range(3 * taps):
            back = 3 * taps - 1 - t
            a, bc = t // taps, t % taps
            wtmp[a * chans : (a + 1) * chans, bc * chans : (bc + 1) * chans] = tall[
                back * chans : (back + 1) * chans, :
            ]
        wall[2 + k] = wtmp[...].astype(BF16)

    for copy in arrivals[2:]:
        copy.wait()
    plain_weight(0, w1_ref)
    plain_weight(1, w2_ref)
    wait_planes(0)

    def layer_one(s):
        build(0, x_zero, ex, s)
        out = conv(0, ex, s)
        pieces = []
        for v in range(EXT):
            pre_one[s, v] = out[v]
            pieces.append((jnp.maximum(out[v], 0.0) * mask[s, v]).astype(BF16))
            hidden[s, v] = pieces[v]
        put_planes(1, s, pieces)

    bricks(0, rounds, layer_one, group)
    send_planes(1)
    flipped_weight(0, w1_ref)
    flipped_weight(1, w2_ref)
    wait_planes(1)

    def layer_two(s):
        build(1, hidden, ey, s)
        out = conv(1, ey, s)
        cot = to_ext([cot_ref[s, :, cut(v)].astype(F32) for v in range(INNER)])
        result, pieces = [], []
        for v in range(EXT):
            pre = out[v] + x_zero[s, v].astype(F32)
            result.append(jnp.maximum(pre, 0.0) * mask[s, v])
            pieces.append(jnp.where(pre > 0.0, cot[v] * mask[s, v], 0.0).astype(BF16))
            grad_two[s, v] = pieces[v]
        for v, piece in enumerate(from_ext(result)):
            res_ref[s, :, cut(v)] = piece.astype(BF16)
        put_planes(2, s, pieces)
        put_grad(s, pieces)

    bricks(0, rounds, layer_two, group)
    send_planes(2)
    departures[0].start()
    weight_term(1, ey)
    sum_scatter(1)
    wait_planes(2)

    def layer_three(s):
        build(2, grad_two, ey, s)
        out = conv(3, ey, s)
        pieces = []
        for v in range(EXT):
            pieces.append(jnp.where(pre_one[s, v] > 0.0, out[v] * mask[s, v], 0.0).astype(BF16))
            grad_one[s, v] = pieces[v]
        put_planes(3, s, pieces)
        put_grad(s, pieces)

    half = rounds // 2
    bricks(0, half, layer_three, group)
    sum_cross(1)
    bricks(half, rounds, layer_three, group)
    send_planes(3)
    weight_term(0, ex)
    sum_scatter(0)
    sum_gather(1)
    wait_planes(3)

    def layer_four(s):
        build(3, grad_one, ey, s)
        out = conv(2, ey, s)
        done = [(out[v] + grad_two[s, v].astype(F32)) * mask[s, v] for v in range(EXT)]
        for v, piece in enumerate(from_ext(done)):
            gf_ref[s, :, cut(v)] = piece.astype(BF16)

    pair = grouping(2)
    third, most = slots // pair // 3, 2 * (slots // pair) // 3
    bricks(0, third, layer_four, pair)
    sum_cross(0)
    bricks(third, most, layer_four, pair)
    sum_gather(0)
    bricks(most, slots // pair, layer_four, pair)
    departures[1].start()
    sum_end(1, g2_ref)
    departures[3].start()
    sum_end(0, g1_ref)
    departures[2].start()
    for step in range(4):
        end_planes(step)
    sum_sent(0)
    sum_sent(1)
    for copy in departures:
        copy.wait()


def body(features, occupancy, neighbours, w_first, w_second, cotangent):
    slots, chans = features.shape[0], features.shape[1]
    n_tx, n_ty = lax.axis_size("tx"), lax.axis_size("ty")
    depth = (EDGE + 1) * chans
    blocks = depth // TILE
    share = -(-blocks // n_ty)
    wide = (slots, EXT, chans, LANES)
    dma = pltpu.SemaphoreType.DMA
    ways_y, ways_x = max(n_ty - 1, 1), max(n_tx - 1, 1)
    in_hbm = pl.BlockSpec(memory_space=pltpu.HBM)
    return pl.pallas_call(
        functools.partial(kernel, n_tx, n_ty),
        out_shape=(
            jax.ShapeDtypeStruct(features.shape, BF16),
            jax.ShapeDtypeStruct(features.shape, BF16),
            jax.ShapeDtypeStruct(w_first.shape, F32),
            jax.ShapeDtypeStruct(w_second.shape, F32),
        ),
        in_specs=[in_hbm] * 6,
        out_specs=(in_hbm,) * 4,
        scratch_shapes=[
            pltpu.VMEM(features.shape, BF16),
            pltpu.VMEM(occupancy.shape, jnp.int32),
            pltpu.SMEM(neighbours.shape, jnp.int32),
            pltpu.VMEM(w_first.shape, BF16),
            pltpu.VMEM(w_second.shape, BF16),
            pltpu.VMEM(cotangent.shape, BF16),
            pltpu.VMEM(features.shape, BF16),
            pltpu.VMEM(features.shape, BF16),
            pltpu.VMEM(w_first.shape, F32),
            pltpu.VMEM(w_second.shape, F32),
            pltpu.VMEM(wide, F32),
            pltpu.VMEM(wide, F32),
            pltpu.VMEM(wide, BF16),
            pltpu.VMEM(wide, BF16),
            pltpu.VMEM(wide, BF16),
            pltpu.VMEM(wide, BF16),
            pltpu.VMEM((slots, depth, EXT * LANES), BF16),
            pltpu.VMEM((slots, depth, EXT * LANES), BF16),
            pltpu.VMEM((slots, 3 * chans, EXT * LANES), BF16),
            pltpu.VMEM((4, 2 * slots, chans, LANES), BF16),
            pltpu.VMEM((4, 2 * slots, chans, LANES), BF16),
            pltpu.VMEM((4, 2 * slots, chans, LANES), BF16),
            pltpu.VMEM((4, 2 * slots, chans, LANES), BF16),
            pltpu.VMEM((4, 3 * chans, depth), BF16),
            pltpu.VMEM((3 * chans, depth), F32),
            pltpu.VMEM((2, share * n_ty, TILE, LANES), F32),
            pltpu.VMEM((2, ways_y, share, TILE, LANES), F32),
            pltpu.VMEM((2, n_tx, share, TILE, LANES), F32),
            pltpu.VMEM((2, share * n_ty, TILE, LANES), F32),
            dma((16,)),
            dma((16,)),
            dma((2, ways_y)),
            dma((2, ways_y)),
            dma((2, ways_x)),
            dma((2, ways_x)),
            dma((2, ways_y)),
            dma((2, ways_y)),
            dma((10,)),
        ],
        compiler_params=pltpu.CompilerParams(
            collective_id=0, has_side_effects=True, vmem_limit_bytes=63 * 1024 * 1024
        ),
    )(features, occupancy, neighbours, w_first, w_second, cotangent)


def solution(mesh):
    return jax.shard_map(
        body,
        mesh=mesh,
        in_specs=(
            P(("tx", "ty"), None, None),
            P(("tx", "ty"), None),
            P(("tx", "ty"), None),
            P(),
            P(),
            P(("tx", "ty"), None, None),
        ),
        out_specs=(P(("tx", "ty"), None, None), P(("tx", "ty"), None, None), P(), P()),
        check_vma=False,
    )
```

```python
import functools
import math

import jax
import jax.numpy as jnp
from jax import lax
from jax.experimental import pallas as pl
from jax.experimental.pallas import tpu as pltpu
from jax.sharding import PartitionSpec as P

EDGE = 8
PLANE = EDGE * EDGE
LANES = 128
EXT = (EDGE + 2) * PLANE // LANES
INNER = EDGE * PLANE // LANES
TILE = 8
MESH = pl.DeviceIdType.MESH
F32 = jnp.float32
BF16 = jnp.bfloat16


def turn(value, shift):
    shift = shift % LANES
    return value if shift == 0 else pltpu.roll(value, shift, 1)


def kernel(
    n_tx, n_ty, feat_in, occ_in, nbr_in, w1_in, w2_in, cot_in,
    res_out, gf_out, g1_out, g2_out,
    feat_ref, occ_ref, nbr_ref, w1_ref, w2_ref, cot_ref, res_ref, gf_ref, g1_ref, g2_ref,
    mask, pre_one, x_zero, hidden, grad_two, grad_one,
    ex, ey, g3, planes_0, planes_1, planes_2, planes_3,
    wall, wtmp,
    terms, parts, cross, total,
    halo_send, halo_recv, ty_send, ty_recv, tx_send, tx_recv, ag_send, ag_recv, local_sem,
):
    arrivals = [
        pltpu.make_async_copy(src, dst, local_sem.at[i])
        for i, (src, dst) in enumerate((
            (occ_in, occ_ref), (feat_in, feat_ref), (nbr_in, nbr_ref),
            (w1_in, w1_ref), (w2_in, w2_ref), (cot_in, cot_ref),
        ))
    ]
    departures = [
        pltpu.make_async_copy(src, dst, local_sem.at[len(arrivals) + i])
        for i, (src, dst) in enumerate((
            (res_ref, res_out), (gf_ref, gf_out), (g1_ref, g1_out), (g2_ref, g2_out),
        ))
    ]
    for copy in arrivals:
        copy.start()
    slots, chans = feat_ref.shape[0], feat_ref.shape[1]
    taps = EDGE + 1
    depth = taps * chans
    tx, ty = lax.axis_index("tx"), lax.axis_index("ty")
    base = (tx * n_ty + ty) * slots
    share = total.shape[1] // n_ty
    used = depth // TILE

    lane = lax.broadcasted_iota(jnp.int32, (chans, LANES), 1)
    low = lane < PLANE
    in_j = (lane // EDGE) % EDGE
    in_k = lane % EDGE
    zero = jnp.zeros((chans, LANES), F32)
    none = jnp.zeros((chans, LANES), BF16)

    def half_mask(where):
        return jnp.where(where, 1.0, 0.0).astype(BF16) > 0

    low_half = half_mask(low)
    j_first, j_last = half_mask(in_j == 0), half_mask(in_j == EDGE - 1)
    k_first, k_last = half_mask(in_k == 0), half_mask(in_k == EDGE - 1)

    def to_ext(pieces):
        turned = [turn(p, PLANE) for p in pieces]
        out = [jnp.where(low, 0.0, turned[0])]
        for v in range(1, INNER):
            out.append(jnp.where(low, turned[v - 1], turned[v]))
        out.append(jnp.where(low, turned[-1], 0.0))
        return out

    def from_ext(pieces):
        turned = [turn(p, PLANE) for p in pieces]
        return [jnp.where(low, turned[v], turned[v + 1]) for v in range(INNER)]

    def cut(v):
        return slice(v * LANES, (v + 1) * LANES)

    planes = [planes_0, planes_1, planes_2, planes_3]
    for ref in planes:
        ref[:, slots:] = jnp.zeros((4, slots, chans, LANES), BF16)
    terms[...] = jnp.zeros(terms.shape, F32)
    barrier = pltpu.get_barrier_semaphore()
    for d in range(1, n_ty):
        pl.semaphore_signal(barrier, inc=1, device_id={"ty": lax.rem(ty + d, n_ty)}, device_id_type=MESH)
    for d in range(1, n_tx):
        pl.semaphore_signal(barrier, inc=1, device_id={"tx": lax.rem(tx + d, n_tx)}, device_id_type=MESH)

    has = [tx > 0, tx < n_tx - 1, ty > 0, ty < n_ty - 1]
    target = [{"tx": tx - 1}, {"tx": tx + 1}, {"ty": ty - 1}, {"ty": ty + 1}]

    def plane_copy(step, face):
        at = step * 4 + face
        return pltpu.make_async_remote_copy(
            src_ref=planes[step].at[face, pl.ds(0, slots)],
            dst_ref=planes[step].at[face, pl.ds(slots, slots)],
            send_sem=halo_send.at[at],
            recv_sem=halo_recv.at[at],
            device_id=target[face],
            device_id_type=MESH,
        )

    def put_planes(step, s, pieces):
        planes[step][0, s] = pieces[0]
        planes[step][1, s] = pieces[EXT - 1]
        near, far = none, none
        for v in range(EXT):
            near = near + turn(jnp.where(j_first, pieces[v], none), EDGE * v)
            far = far + turn(jnp.where(j_last, pieces[v], none), EDGE * v + EDGE)
        planes[step][2, s] = near
        planes[step][3, s] = far

    def send_planes(step):
        for face in range(4):
            @pl.when(has[face])
            def _():
                plane_copy(step, face).start()

    def wait_planes(step):
        for face in range(4):
            @pl.when(has[face])
            def _():
                plane_copy(step, face ^ 1).wait_recv()

    def end_planes(step):
        for face in range(4):
            @pl.when(has[face])
            def _():
                plane_copy(step, face).wait_send()

    offsets = [-n_ty * slots, n_ty * slots, -slots, slots]

    def halo(step, s, face):
        ident = nbr_ref[s, face]
        own = ident - base
        local = (own >= 0) & (own < slots)
        pick = jnp.where(local, own, own - offsets[face] + slots)
        pick = jnp.clip(pick, 0, 2 * slots - 1)
        return planes[step][face ^ 1, pick] * live(ident)

    def live(ident):
        return jnp.full((chans, LANES), jnp.where(ident >= 0, 1.0, 0.0), F32).astype(BF16)

    def build(step, field, cols, s):
        ext = [field[s, v] for v in range(EXT)]
        ext[0] = ext[0] + halo(step, s, 0)
        ext[EXT - 1] = ext[EXT - 1] + halo(step, s, 1)
        before, after = halo(step, s, 2), halo(step, s, 3)
        ident = [nbr_ref[s, 4], nbr_ref[s, 5]]
        pick = [jnp.clip(i - base, 0, slots - 1) for i in ident]
        there = [live(i) for i in ident]
        for v in range(EXT):
            down = field[pick[0], v] * there[0]
            up = field[pick[1], v] * there[1]
            rows = [
                jnp.where(j_first, turn(before, -(PLANE + EDGE * v)), turn(ext[v], EDGE)),
                ext[v],
                jnp.where(j_last, turn(after, PLANE - EDGE - EDGE * v), turn(ext[v], -EDGE)),
            ]
            outside = [j_first, None, j_last]
            for b in range(3):
                step_j = EDGE * (1 - b)
                first = turn(down, step_j - (EDGE - 1))
                last = turn(up, step_j + (EDGE - 1))
                if outside[b] is not None:
                    first = jnp.where(outside[b], none, first)
                    last = jnp.where(outside[b], none, last)
                trio = [
                    jnp.where(k_first, first, turn(rows[b], 1)),
                    rows[b],
                    jnp.where(k_last, last, turn(rows[b], -1)),
                ]
                for c in range(3):
                    at = (b * 3 + c) * chans
                    cols[s, at : at + chans, cut(v)] = trio[c]

    def conv(which, cols, s):
        out = jnp.dot(wall[which], cols[s], preferred_element_type=F32)
        part = [[out[a * chans : (a + 1) * chans, cut(v)] for v in range(EXT)] for a in range(3)]
        lead = [turn(p, PLANE) for p in part[0]]
        tail = [turn(p, PLANE) for p in part[2]]
        return [
            part[1][v]
            + jnp.where(low, lead[v - 1] if v > 0 else zero, lead[v])
            + jnp.where(low, tail[v], tail[v + 1] if v < EXT - 1 else zero)
            for v in range(EXT)
        ]

    def put_grad(s, pieces):
        turned = [turn(p, PLANE) for p in pieces]
        for v in range(EXT):
            ahead = jnp.where(low_half, turned[v], turned[v + 1] if v < EXT - 1 else none)
            behind = jnp.where(low_half, turned[v - 1] if v > 0 else none, turned[v])
            g3[s, 0:chans, cut(v)] = ahead
            g3[s, chans : 2 * chans, cut(v)] = pieces[v]
            g3[s, 2 * chans : 3 * chans, cut(v)] = behind

    group = 3 if slots % 3 == 0 else 1

    def bricks(start, stop, one, between=None):
        def several(g, carry):
            for i in range(group):
                one(g * group + i)
            if between is not None:
                pl.when(g == (start + stop - 1) // 2)(between)
            return carry

        lax.fori_loop(start, stop, several, 0)

    rounds = slots // group

    def weight_term(which, cols):
        def one(s, acc):
            return acc + lax.dot_general(
                cols[s], g3[s], (((1,), (1,)), ((), ())), preferred_element_type=F32
            )

        acc = lax.fori_loop(0, slots, one, jnp.zeros((depth, 3 * chans), F32))
        terms[which, 0:used, :, 0 : 3 * chans] = acc.reshape(used, TILE, 3 * chans)

    def scatter_copy(k, d):
        to = lax.rem(ty + d, n_ty)
        return pltpu.make_async_remote_copy(
            src_ref=terms.at[k, pl.ds(to * share, share)],
            dst_ref=parts.at[k, d - 1],
            send_sem=ty_send.at[k, d - 1],
            recv_sem=ty_recv.at[k, d - 1],
            device_id={"ty": to},
            device_id_type=MESH,
        )

    def cross_copy(k, d):
        return pltpu.make_async_remote_copy(
            src_ref=cross.at[k, tx],
            dst_ref=cross.at[k, tx],
            send_sem=tx_send.at[k, d - 1],
            recv_sem=tx_recv.at[k, d - 1],
            device_id={"tx": lax.rem(tx + d, n_tx)},
            device_id_type=MESH,
        )

    def gather_copy(k, d):
        mine = pl.ds(ty * share, share)
        return pltpu.make_async_remote_copy(
            src_ref=total.at[k, mine],
            dst_ref=total.at[k, mine],
            send_sem=ag_send.at[k, d - 1],
            recv_sem=ag_recv.at[k, d - 1],
            device_id={"ty": lax.rem(ty + d, n_ty)},
            device_id_type=MESH,
        )

    def sum_scatter(k):
        for d in range(1, n_ty):
            scatter_copy(k, d).start()

    def sum_cross(k):
        for d in range(1, n_ty):
            scatter_copy(k, d).wait_recv()
        acc = terms[k, pl.ds(ty * share, share)]
        for d in range(1, n_ty):
            acc = acc + parts[k, d - 1]
        cross[k, tx] = acc
        for d in range(1, n_tx):
            cross_copy(k, d).start()

    def sum_gather(k):
        for d in range(1, n_tx):
            cross_copy(k, d).wait_recv()
        acc = cross[k, 0]
        for i in range(1, n_tx):
            acc = acc + cross[k, i]
        total[k, pl.ds(ty * share, share)] = acc
        for d in range(1, n_ty):
            gather_copy(k, d).start()

    scale = 1.0 / math.sqrt(slots * n_tx * n_ty * EDGE * PLANE)

    def sum_end(k, out_ref):
        for d in range(1, n_ty):
            gather_copy(k, d).wait_recv()
        whole = total[k, 0:used].reshape(depth, LANES).T
        for a in range(3):
            out_ref[:, a * depth : (a + 1) * depth] = whole[a * chans : (a + 1) * chans, :] * scale

    def sum_sent(k):
        for d in range(1, n_ty):
            scatter_copy(k, d).wait_send()
            gather_copy(k, d).wait_send()
        for d in range(1, n_tx):
            cross_copy(k, d).wait_send()

    def first(s):
        pieces = to_ext([feat_ref[s, :, cut(v)].astype(F32) for v in range(INNER)])
        pieces = [(p * mask[s, v]).astype(BF16) for v, p in enumerate(pieces)]
        for v in range(EXT):
            x_zero[s, v] = pieces[v]
        put_planes(0, s, pieces)

    arrivals[0].wait()
    for s in range(slots):
        holes = to_ext([
            jnp.broadcast_to(occ_ref[s : s + 1, cut(v)].astype(F32), (chans, LANES))
            for v in range(INNER)
        ])
        for v in range(EXT):
            mask[s, v] = holes[v]
    arrivals[1].wait()
    bricks(0, rounds, first)
    pl.semaphore_wait(barrier, n_ty - 1 + n_tx - 1)
    send_planes(0)

    def plain_weight(k, ref):
        wide = ref[...].astype(F32)
        for a in range(3):
            wall[k, a * chans : (a + 1) * chans, :] = wide[:, a * depth : (a + 1) * depth].astype(BF16)

    def flipped_weight(k, ref):
        tall = ref[...].astype(F32).T
        for t in range(3 * taps):
            back = 3 * taps - 1 - t
            a, bc = t // taps, t % taps
            wtmp[a * chans : (a + 1) * chans, bc * chans : (bc + 1) * chans] = tall[
                back * chans : (back + 1) * chans, :
            ]
        wall[2 + k] = wtmp[...].astype(BF16)

    for copy in arrivals[2:]:
        copy.wait()
    plain_weight(0, w1_ref)
    plain_weight(1, w2_ref)
    wait_planes(0)

    def layer_one(s):
        build(0, x_zero, ex, s)
        out = conv(0, ex, s)
        pieces = []
        for v in range(EXT):
            pre_one[s, v] = out[v]
            pieces.append((jnp.maximum(out[v], 0.0) * mask[s, v]).astype(BF16))
            hidden[s, v] = pieces[v]
        put_planes(1, s, pieces)

    bricks(0, rounds, layer_one)
    send_planes(1)
    flipped_weight(0, w1_ref)
    flipped_weight(1, w2_ref)
    wait_planes(1)

    def layer_two(s):
        build(1, hidden, ey, s)
        out = conv(1, ey, s)
        cot = to_ext([cot_ref[s, :, cut(v)].astype(F32) for v in range(INNER)])
        result, pieces = [], []
        for v in range(EXT):
            pre = out[v] + x_zero[s, v].astype(F32)
            result.append(jnp.maximum(pre, 0.0) * mask[s, v])
            pieces.append(jnp.where(pre > 0.0, cot[v] * mask[s, v], 0.0).astype(BF16))
            grad_two[s, v] = pieces[v]
        for v, piece in enumerate(from_ext(result)):
            res_ref[s, :, cut(v)] = piece.astype(BF16)
        put_planes(2, s, pieces)
        put_grad(s, pieces)

    bricks(0, rounds, layer_two)
    send_planes(2)
    departures[0].start()
    weight_term(1, ey)
    sum_scatter(1)
    wait_planes(2)

    def layer_three(s):
        build(2, grad_two, ey, s)
        out = conv(3, ey, s)
        pieces = []
        for v in range(EXT):
            pieces.append(jnp.where(pre_one[s, v] > 0.0, out[v] * mask[s, v], 0.0).astype(BF16))
            grad_one[s, v] = pieces[v]
        put_planes(3, s, pieces)
        put_grad(s, pieces)

    bricks(0, rounds, layer_three)
    send_planes(3)
    weight_term(0, ex)
    sum_scatter(0)
    sum_cross(1)
    wait_planes(3)

    def layer_four(s):
        build(3, grad_one, ey, s)
        out = conv(2, ey, s)
        done = [(out[v] + grad_two[s, v].astype(F32)) * mask[s, v] for v in range(EXT)]
        for v, piece in enumerate(from_ext(done)):
            gf_ref[s, :, cut(v)] = piece.astype(BF16)

    def sums_on():
        sum_cross(0)
        sum_gather(1)

    bricks(0, rounds, layer_four, sums_on)
    departures[1].start()
    sum_gather(0)
    sum_end(1, g2_ref)
    departures[3].start()
    sum_end(0, g1_ref)
    departures[2].start()
    for step in range(4):
        end_planes(step)
    sum_sent(0)
    sum_sent(1)
    for copy in departures:
        copy.wait()


def body(features, occupancy, neighbours, w_first, w_second, cotangent):
    slots, chans = features.shape[0], features.shape[1]
    n_tx, n_ty = lax.axis_size("tx"), lax.axis_size("ty")
    depth = (EDGE + 1) * chans
    blocks = depth // TILE
    share = -(-blocks // n_ty)
    wide = (slots, EXT, chans, LANES)
    dma = pltpu.SemaphoreType.DMA
    ways_y, ways_x = max(n_ty - 1, 1), max(n_tx - 1, 1)
    in_hbm = pl.BlockSpec(memory_space=pltpu.HBM)
    return pl.pallas_call(
        functools.partial(kernel, n_tx, n_ty),
        out_shape=(
            jax.ShapeDtypeStruct(features.shape, BF16),
            jax.ShapeDtypeStruct(features.shape, BF16),
            jax.ShapeDtypeStruct(w_first.shape, F32),
            jax.ShapeDtypeStruct(w_second.shape, F32),
        ),
        in_specs=[in_hbm] * 6,
        out_specs=(in_hbm,) * 4,
        scratch_shapes=[
            pltpu.VMEM(features.shape, BF16),
            pltpu.VMEM(occupancy.shape, jnp.int32),
            pltpu.SMEM(neighbours.shape, jnp.int32),
            pltpu.VMEM(w_first.shape, BF16),
            pltpu.VMEM(w_second.shape, BF16),
            pltpu.VMEM(cotangent.shape, BF16),
            pltpu.VMEM(features.shape, BF16),
            pltpu.VMEM(features.shape, BF16),
            pltpu.VMEM(w_first.shape, F32),
            pltpu.VMEM(w_second.shape, F32),
            pltpu.VMEM(wide, F32),
            pltpu.VMEM(wide, F32),
            pltpu.VMEM(wide, BF16),
            pltpu.VMEM(wide, BF16),
            pltpu.VMEM(wide, BF16),
            pltpu.VMEM(wide, BF16),
            pltpu.VMEM((slots, depth, EXT * LANES), BF16),
            pltpu.VMEM((slots, depth, EXT * LANES), BF16),
            pltpu.VMEM((slots, 3 * chans, EXT * LANES), BF16),
            pltpu.VMEM((4, 2 * slots, chans, LANES), BF16),
            pltpu.VMEM((4, 2 * slots, chans, LANES), BF16),
            pltpu.VMEM((4, 2 * slots, chans, LANES), BF16),
            pltpu.VMEM((4, 2 * slots, chans, LANES), BF16),
            pltpu.VMEM((4, 3 * chans, depth), BF16),
            pltpu.VMEM((3 * chans, depth), F32),
            pltpu.VMEM((2, share * n_ty, TILE, LANES), F32),
            pltpu.VMEM((2, ways_y, share, TILE, LANES), F32),
            pltpu.VMEM((2, n_tx, share, TILE, LANES), F32),
            pltpu.VMEM((2, share * n_ty, TILE, LANES), F32),
            dma((16,)),
            dma((16,)),
            dma((2, ways_y)),
            dma((2, ways_y)),
            dma((2, ways_x)),
            dma((2, ways_x)),
            dma((2, ways_y)),
            dma((2, ways_y)),
            dma((10,)),
        ],
        compiler_params=pltpu.CompilerParams(
            collective_id=0, has_side_effects=True, vmem_limit_bytes=63 * 1024 * 1024
        ),
    )(features, occupancy, neighbours, w_first, w_second, cotangent)


def solution(mesh):
    return jax.shard_map(
        body,
        mesh=mesh,
        in_specs=(
            P(("tx", "ty"), None, None),
            P(("tx", "ty"), None),
            P(("tx", "ty"), None),
            P(),
            P(),
            P(("tx", "ty"), None, None),
        ),
        out_specs=(P(("tx", "ty"), None, None), P(("tx", "ty"), None, None), P(), P()),
        check_vma=False,
    )
```
